32 devices in a mesh: dp: 2 (over x), seq: 4 (over y, core), tensor: 4 (over z).
Axes of the slice: x: 2, y: 2, z: 4, core: 2. Of those that a mesh axis runs over, the one named last changes fastest.
Arguments:
- tokens: bfloat16 [2, 4, 1024, 1536], P(None, 'dp', 'seq'), may hold values from -6 to 6
- segment_ids: int32 [2, 4, 1024], P(None, 'dp'), may hold values from 0 to 4, as said below
- cotangent: bfloat16 [2, 4, 1024, 1536], P(None, 'dp', 'seq'), may hold values from -6 to 6
- in_gain: bfloat16 [1536], P(('dp', 'seq')), may hold values from 0.5 to 1.5
- z_proj: bfloat16 [1536, 3072], P(('dp', 'seq'), 'tensor'), may hold values from -0.15625 to 0.15625
- x_proj: bfloat16 [1536, 3072], P(('dp', 'seq'), 'tensor'), may hold values from -0.15625 to 0.15625
- bc_proj: bfloat16 [1536, 256], P(('dp', 'seq'), 'tensor'), may hold values from -0.15625 to 0.15625
- dt_proj: bfloat16 [1536, 48], P(('dp', 'seq'), 'tensor'), may hold values from -0.078125 to 0.078125
- out_proj: bfloat16 [3072, 1536], P('tensor', ('dp', 'seq')), may hold values from -0.109375 to 0.109375
- conv_x: float32 [4, 3072], P(None, 'tensor'), may hold values from -3 to 3
- conv_x_bias: float32 [3072], P('tensor'), may hold values from -1.5 to 1.5
- conv_bc: float32 [4, 256], P(None, 'tensor'), may hold values from -3 to 3
- conv_bc_bias: float32 [256], P('tensor'), may hold values from -1.5 to 1.5
- dt_bias: float32 [48], P('tensor'), may hold values from -2.5 to -1
- decay_rate: float32 [48], P('tensor'), may hold values from 0.002 to 0.25
- skip_gain: float32 [48], P('tensor'), may hold values from 0.5 to 1.5
- out_gain: float32 [3072], P('tensor'), may hold values from 0.5 to 1.5
Outputs:
- output: bfloat16 [2, 4, 1024, 1536], P(None, 'dp', 'seq')
- token_grad: float32 [2, 4, 1024, 1536], P(None, 'dp', 'seq')
- in_gain_grad: float32 [1536], P(('dp', 'seq'))
- z_proj_grad: float32 [1536, 3072], P(('dp', 'seq'), 'tensor')
- x_proj_grad: float32 [1536, 3072], P(('dp', 'seq'), 'tensor')
- bc_proj_grad: float32 [1536, 256], P(('dp', 'seq'), 'tensor')
- dt_proj_grad: float32 [1536, 48], P(('dp', 'seq'), 'tensor')
- out_proj_grad: float32 [3072, 1536], P('tensor', ('dp', 'seq'))
- conv_x_grad: float32 [4, 3072], P(None, 'tensor')
- conv_x_bias_grad: float32 [3072], P('tensor')
- conv_bc_grad: float32 [4, 256], P(None, 'tensor')
- conv_bc_bias_grad: float32 [256], P('tensor')
- dt_bias_grad: float32 [48], P('tensor')
- decay_rate_grad: float32 [48], P('tensor')
- skip_gain_grad: float32 [48], P('tensor')
- out_gain_grad: float32 [3072], P('tensor')
The draws below stay inside these ranges and needn't reach their ends.
Inputs may be any that keep to these rules, and one draw needn't show every extreme that they name: `segment_ids`: within each row the ids never fall, and the row's first token has id 0.
All inputs are finite; a program needn't handle non-finite values.
Results may differ from the reference program's by a relative error of at most 0.022.
Values may be sent and summed in bfloat16 or wider, within the bound.
No kernel may reach another device: no remote copies, remote signals or barrier semaphores. Data moves between devices by JAX's collectives and lax.ppermute only.
A program may use at most 192 MiB of HBM per device.

```python
import math
import jax
import jax.numpy as jnp
from jax import lax

D = 1536
DI = 3072
NH = 48
HD = 64
NS = 128
KW = 4
STRETCH = 256
MICRO = 2
ROWS_DEV = 2
ROWS = 4
LEN = 1024


def draw_segment_ids(key, part):
    key = jax.random.fold_in(key, 11)
    subkeys = jax.random.split(key, 7)
    group_size = MICRO * ROWS_DEV
    dp_count = ROWS // ROWS_DEV
    quarter_len = LEN // 4
    chosen_slot = jnp.repeat(jax.random.randint(subkeys[0], (dp_count,), 0, group_size), ROWS_DEV)[None, :]
    slot_index = jnp.arange(MICRO, dtype=jnp.int32)[:, None] * ROWS_DEV + jnp.arange(ROWS, dtype=jnp.int32)[None, :] % ROWS_DEV
    spanning = (slot_index == chosen_slot)[:, :, None]
    fullest = (slot_index == (chosen_slot + 1) % group_size)[:, :, None]
    bound_slot = jnp.arange(4, dtype=jnp.int32)
    doc_counts = jax.random.randint(subkeys[1], (MICRO, ROWS, 1), 0, 5)
    spread_bounds = jax.random.randint(subkeys[2], (MICRO, ROWS, 4), 1, LEN)
    free_bounds = jnp.where(bound_slot < doc_counts, spread_bounds, LEN)
    head_bound = jax.random.randint(subkeys[3], (MICRO, ROWS, 1), 1, STRETCH)
    tail_bound = jax.random.randint(subkeys[4], (MICRO, ROWS, 1), LEN - STRETCH + 1, LEN)
    coin_flips = jax.random.randint(subkeys[5], (MICRO, ROWS, 2), 0, 2)
    edge_pair = jnp.concatenate([jnp.where(coin_flips[..., :1] == 1, head_bound, LEN), jnp.where(coin_flips[..., 1:] == 1, tail_bound, LEN)], axis=-1)
    span_bounds = jnp.concatenate([edge_pair, jnp.full((MICRO, ROWS, 2), LEN, jnp.int32)], axis=-1)
    offsets = jax.random.randint(subkeys[6], (MICRO, ROWS, 4), 0, quarter_len)
    full_bounds = jnp.maximum(jnp.where(bound_slot == 1, quarter_len, bound_slot * quarter_len + offsets), 1)
    bounds = jnp.where(spanning, span_bounds, jnp.where(fullest, full_bounds, free_bounds))
    position = jnp.arange(LEN, dtype=jnp.int32)
    return jnp.sum((position[None, None, None, :] >= bounds[..., None]).astype(jnp.int32), axis=2)


def level_of(key, dims, cuts, least, largest):
    factor_of, own = 1.0, jax.random.fold_in(key, 6)
    for dim, shards_of in cuts:
        heights = jnp.exp(jax.random.uniform(jax.random.fold_in(own, dim), (shards_of,), jnp.float32, least / len(cuts), largest / len(cuts)))
        factor_of = factor_of * jnp.repeat(heights, dims[dim] // shards_of).reshape([-1 if axis == dim else 1 for axis in range(len(dims))])
    return factor_of


def normal_values(stream_key, dims, scale, most, cuts=(), kind=jnp.bfloat16):
    level = level_of(stream_key, dims, cuts, -0.22, 0.18) if cuts else 1.0
    values = jax.random.normal(stream_key, dims, jnp.float32) * scale * level
    return jnp.minimum(jnp.maximum(values, -most), most).astype(kind)


def setup_inputs(seed: int = 0) -> dict:
    arg_keys = jax.random.split(jax.random.key(seed), 18)
    return {
        "tokens": normal_values(arg_keys[0], (MICRO, ROWS, LEN, D), 1.0, 6.0, ((1, 2), (2, 4))),
        "segment_ids": draw_segment_ids(jax.random.fold_in(arg_keys[17], 71), 0),
        "cotangent": normal_values(arg_keys[2], (MICRO, ROWS, LEN, D), 1.0, 6.0, ((1, 2), (2, 4))),
        "in_gain": jnp.clip(1.0 + 0.1 * jax.random.normal(arg_keys[3], (D,), jnp.float32), 0.5, 1.5).astype(jnp.bfloat16),
        "z_proj": normal_values(arg_keys[4], (D, DI), D ** -0.5, 0.15625, ((0, 8), (1, 4))),
        "x_proj": normal_values(arg_keys[5], (D, DI), D ** -0.5, 0.15625, ((0, 8), (1, 4))),
        "bc_proj": normal_values(arg_keys[6], (D, 2 * NS), D ** -0.5, 0.15625, ((0, 8), (1, 4))),
        "dt_proj": normal_values(arg_keys[7], (D, NH), (4 * D) ** -0.5, 0.078125, ((0, 8), (1, 4))),
        "out_proj": normal_values(arg_keys[8], (DI, D), DI ** -0.5, 0.109375, ((0, 4), (1, 8))),
        "conv_x": normal_values(arg_keys[9], (KW, DI), KW ** -0.5, 3.0, ((1, 4),), jnp.float32),
        "conv_x_bias": normal_values(arg_keys[10], (DI,), 0.3, 1.5, ((0, 4),), jnp.float32),
        "conv_bc": normal_values(arg_keys[11], (KW, 2 * NS), KW ** -0.5, 3.0, ((1, 4),), jnp.float32),
        "conv_bc_bias": normal_values(arg_keys[12], (2 * NS,), 0.3, 1.5, ((0, 4),), jnp.float32),
        "dt_bias": jnp.clip(-2.5 + 1.5 * jax.random.uniform(arg_keys[13], (NH,), jnp.float32) ** level_of(arg_keys[13], (NH,), ((0, 4),), -0.2, 0.2), -2.5, -1.0),
        "decay_rate": jnp.clip(jnp.exp(math.log(0.25) - 4.828314 * jax.random.uniform(arg_keys[14], (NH,), jnp.float32) ** level_of(arg_keys[14], (NH,), ((0, 4),), -0.2, 0.2)), 0.002, 0.25),
        "skip_gain": jnp.clip(1.0 + 0.1 * jax.random.normal(arg_keys[15], (NH,), jnp.float32), 0.5, 1.5),
        "out_gain": jnp.clip(1.0 + 0.1 * jax.random.normal(arg_keys[16], (DI,), jnp.float32), 0.5, 1.5),
    }


@jax.custom_vjp
def low(v):
    return lax.optimization_barrier(v.astype(jnp.bfloat16)).astype(jnp.float32)

@jax.custom_vjp
def low_back(v):
    return v

def low_keep(v):
    return (low(v), None)

def low_pass(kept, grad):
    return (grad,)

def back_keep(v):
    return (v, None)

def back_low(kept, grad):
    return (low(grad),)
low.defvjp(low_keep, low_pass)
low_back.defvjp(back_keep, back_low)
eps = 1e-05
highest = lax.Precision.HIGHEST

def rms_scale(values, gain_vec):
    return values * lax.rsqrt(lax.optimization_barrier(jnp.mean(values * values, axis=-1, keepdims=True)) + eps) * gain_vec

def project(values, matrix):
    return jnp.matmul(values, matrix, precision=highest)

def causal_conv(values, weight, bias_vec, seg_rows):
    length = values.shape[1]
    padded = jnp.pad(values, ((0, 0), (KW - 1, 0), (0, 0)))
    padded_seg = jnp.pad(seg_rows, ((0, 0), (KW - 1, 0)), constant_values=-1)
    result = bias_vec + jnp.zeros_like(values)
    for offset in range(KW):
        keep_mask = (padded_seg[:, offset:offset + length] == seg_rows).astype(jnp.float32)
        result = result + weight[offset] * padded[:, offset:offset + length] * keep_mask[:, :, None]
    return result

def stretch_step(state_now, stretch_data):
    x_heads, b_mat, c_mat, step_sizes, rates, seg_here, seg_before = stretch_data
    cumulative = jnp.cumsum(rates, axis=0)
    length = seg_here.shape[0]
    causal_pairs = jnp.arange(length)[:, None] >= jnp.arange(length)[None, :]
    pair_mask = ((seg_here[:, None] == seg_here[None, :]) & causal_pairs)[None]
    cum_heads = cumulative.T
    log_gap = cum_heads[:, :, None] - cum_heads[:, None, :]
    pair_weights = jnp.where(pair_mask, jnp.exp(jnp.where(pair_mask, log_gap, 0.0)), 0.0) * step_sizes.T[:, None, :]
    scores = jnp.matmul(c_mat, b_mat.T, precision=highest)
    mixing = low(low_back(jnp.broadcast_to(scores, pair_weights.shape)) * pair_weights)
    intra_out = jnp.einsum('hts,shp->thp', mixing, x_heads, precision=highest)
    end_weights = jnp.where((seg_here == seg_here[-1])[:, None], jnp.exp(cumulative[-1:] - cumulative), 0.0) * step_sizes
    weighted = low(x_heads * end_weights[:, :, None])
    local_state = jnp.einsum('shp,sn->hpn', weighted, b_mat, precision=highest)
    entry_decay = jnp.where((seg_here == seg_before)[:, None], jnp.exp(cumulative), 0.0)
    carried = jnp.einsum('tn,hpn->thp', c_mat, state_now, precision=highest) * entry_decay[:, :, None]
    chain_decay = jnp.where(seg_here[-1] == seg_before, jnp.exp(cumulative[-1]), 0.0)
    next_state = chain_decay[:, None, None] * state_now + local_state
    return (next_state, intra_out + carried)

def ssd_row(x_heads, b_mat, c_mat, step_sizes, rates, seg_row):
    stretch_count = seg_row.shape[0] // STRETCH
    seg_stretches = seg_row.reshape(stretch_count, STRETCH)
    seg_before = jnp.concatenate([jnp.full((1,), -1, jnp.int32), seg_stretches[:-1, -1].astype(jnp.int32)])
    stretch_data = (x_heads.reshape(stretch_count, STRETCH, NH, HD), b_mat.reshape(stretch_count, STRETCH, NS), c_mat.reshape(stretch_count, STRETCH, NS), step_sizes.reshape(stretch_count, STRETCH, NH), rates.reshape(stretch_count, STRETCH, NH), seg_stretches, seg_before)
    zero_state = jnp.zeros((NH, HD, NS), jnp.float32)
    _, result = lax.scan(jax.checkpoint(stretch_step), zero_state, stretch_data)
    return result.reshape(seg_row.shape[0], NH, HD)

def forward(tokens, in_gain, z_proj, x_proj, bc_proj, dt_proj, out_proj, conv_x, conv_x_bias, conv_bc, conv_bc_bias, dt_bias, decay_rate, skip_gain, out_gain, seg_rows):
    normed = low(rms_scale(tokens, in_gain))
    gate_z = low_back(project(normed, z_proj))
    x_pre = low_back(low(project(normed, x_proj)))
    bc_pre = low_back(low(project(normed, bc_proj)))
    dt_raw = low_back(project(normed, dt_proj))
    x_act = low(jax.nn.silu(causal_conv(x_pre, conv_x, conv_x_bias, seg_rows)))
    bc_act = low(jax.nn.silu(causal_conv(bc_pre, conv_bc, conv_bc_bias, seg_rows)))
    step_sizes = jax.nn.softplus(dt_raw + dt_bias)
    rates = -decay_rate * step_sizes
    row_count, length = seg_rows.shape
    x_heads = x_act.reshape(row_count, length, NH, HD)
    scanned = jax.vmap(ssd_row)(x_heads, bc_act[..., :NS], bc_act[..., NS:], step_sizes, rates, seg_rows)
    ssd_out = low_back(scanned + skip_gain[:, None] * x_heads).reshape(row_count, length, DI)
    gated = ssd_out * jax.nn.silu(gate_z)
    g_norm = low(rms_scale(gated, out_gain))
    return tokens + project(g_norm, out_proj)

def reference(tokens, segment_ids, cotangent, in_gain, z_proj, x_proj, bc_proj, dt_proj, out_proj, conv_x, conv_x_bias, conv_bc, conv_bc_bias, dt_bias, decay_rate, skip_gain, out_gain):
    micro_count, row_count, length, model_width = tokens.shape
    seg_rows = segment_ids.reshape(micro_count * row_count, length).astype(jnp.int32)
    flat = tokens.reshape(micro_count * row_count, length, model_width).astype(jnp.float32)
    params = [p.astype(jnp.float32) for p in (in_gain, z_proj, x_proj, bc_proj, dt_proj, out_proj, conv_x, conv_x_bias, conv_bc, conv_bc_bias, dt_bias, decay_rate, skip_gain, out_gain)]

    def wrapped(*inputs):
        return forward(*inputs, seg_rows)
    mixed_out, pullback = jax.vjp(wrapped, flat, *params)
    all_grads = pullback(cotangent.reshape(flat.shape).astype(jnp.float32))
    return (mixed_out.astype(jnp.bfloat16).reshape(tokens.shape), all_grads[0].reshape(tokens.shape), all_grads[1], all_grads[2], all_grads[3], all_grads[4], all_grads[5], all_grads[6], all_grads[7], all_grads[8], all_grads[9], all_grads[10], all_grads[11], all_grads[12], all_grads[13], all_grads[14])
```

```python
import functools

import jax
import jax.numpy as jnp
from jax import lax
from jax.experimental import pallas as pl
from jax.experimental.pallas import tpu as pltpu
from jax.sharding import PartitionSpec as P

DI = 3072
D_MODEL = 1536
HD = 64
NS = 128
KW = 4
GHOST = 16
LANES = 128
FIRST = GHOST - KW + 1
AT_END, AT_ENTRY, SEG = KW, KW + 1, KW + 2

eps = 1e-05
F32 = jnp.float32
BF16 = jnp.bfloat16


def dot_nn(a, b):
    return lax.dot_general(a, b, (((1,), (0,)), ((), ())), preferred_element_type=F32)


def dot_nt(a, b):
    return lax.dot_general(a, b, (((1,), (1,)), ((), ())), preferred_element_type=F32)


def pair_route(mask, seq_mask):
    count = lax.axis_size("seq")
    route = []
    for x in range(lax.axis_size("dp")):
        for s in range(count):
            flip_x, flip_y = mask if s % 2 == 0 else seq_mask
            route.append((x * count + s, (x ^ flip_x) * count + (s ^ flip_y)))
    return route


ALONG_X, ALONG_Y = (1, 0), (0, 2)


def cross_first(value):
    return lax.ppermute(value, ("dp", "seq"), pair_route(ALONG_X, ALONG_Y))


def cross_second(value):
    return lax.ppermute(value, ("dp", "seq"), pair_route(ALONG_Y, ALONG_X))


def swap(value, axis, mask):
    return lax.ppermute(value, axis, [(i, i ^ mask) for i in range(lax.axis_size(axis))])


def is_grid():
    return lax.axis_size("dp") == 2 and lax.axis_size("seq") == 4


def chunk_places():
    if not is_grid():
        return jnp.arange(lax.axis_size("dp") * lax.axis_size("seq"), dtype=jnp.int32)
    x = lax.axis_index("dp")
    y = lax.axis_index("seq") // 2
    core = lax.axis_index("seq") % 2
    places = []
    for c in (core, 1 - core):
        for first, second in ((0, 0), (1, 0), (0, 1), (1, 1)):
            flip_x = jnp.where(c == 0, first, second)
            flip_y = jnp.where(c == 0, second, first)
            places.append((x ^ flip_x) * 4 + (y ^ flip_y) * 2 + c)
    return jnp.stack(places).astype(jnp.int32)


def gather_chunks(shard, came, *tokens, late=None):
    if not is_grid():
        every = lax.all_gather(shard, ("dp", "seq"), axis=0)
        return (every,), every
    two = after(jnp.stack([shard, came]), *tokens)
    far = cross_second(two)
    four = jnp.concatenate([two, far if late is None else after(far, late)])
    return (four, swap(four, "seq", 1)), far


def plus(kept, came):
    return kept.astype(F32) + came.astype(F32)


def sum_cores(theirs, mine):
    if not is_grid():
        total = lax.psum_scatter(
            mine.reshape((-1,) + mine.shape[2:]),
            ("dp", "seq"),
            scatter_dimension=0,
            tiled=True,
        ).astype(F32)
        return total, total
    came = swap(theirs, "seq", 1)
    return plus(mine[:2], came[:2]), plus(mine[2:], came[2:]).astype(BF16)


def sum_second(kept, away):
    if not is_grid():
        return kept, away
    came = cross_second(away)
    return plus(kept[0], came[0]), plus(kept[1], came[1]).astype(BF16)


def sum_first(kept, away):
    return plus(kept, cross_first(away)) if is_grid() else kept


def small_sum(value, axes):
    for axis in axes:
        mask = 1
        while mask < lax.axis_size(axis):
            value = value + swap(value, axis, mask)
            mask *= 2
    return value


def fetch_tensor(value):
    count = lax.axis_size("tensor")
    return [
        lax.ppermute(value, "tensor", [(i, (i + step) % count) for i in range(count)])
        for step in range(1, count)
    ]


def sum_tensor(pieces, shared):
    count = lax.axis_size("tensor")
    me = lax.axis_index("tensor")
    rows, width = pieces.shape[1:]
    flat = shared.reshape(-1, width)
    total = lax.dynamic_index_in_dim(pieces, me, 0, keepdims=False)
    every = [flat]
    for step in range(1, count):
        away = lax.dynamic_index_in_dim(pieces, (me + step) % count, 0, keepdims=False)
        route = [(i, (i + step) % count) for i in range(count)]
        came = lax.ppermute(jnp.concatenate([away, flat]), "tensor", route)
        total = total + came[:rows]
        every.append(came[rows:])
    order = (me - jnp.arange(count)) % count
    pick = (order[:, None] == jnp.arange(count)[None]).astype(F32)
    every = jnp.stack(every)
    found = 0.0
    for j in range(count):
        found = found + jnp.sum(pick[j][:, None, None] * every, axis=0)
    return total, found.reshape(shared.shape)


def state_scan(decay, local, backward, tokens=()):
    count = lax.axis_size("seq")
    state = jnp.zeros_like(local)
    leaving = local
    for hop in range(count - 1):
        pair = (count - 1 - hop, count - 2 - hop) if backward else (hop, hop + 1)
        came = lax.ppermute(leaving.astype(BF16), "seq", [pair])
        if hop < len(tokens) and tokens[hop] is not None:
            came = after(came, tokens[hop])
        state = state + came.astype(F32)
        leaving = decay * state + local
    return state.astype(BF16), leaving


def after(value, *tokens):
    return lax.optimization_barrier((value,) + tokens)[0]


def in_turn(me, tokens, work):
    turn = after(me, *tokens)[0] >= 0
    shapes = jax.eval_shape(work)
    return lax.cond(
        turn, work, lambda: jax.tree.map(lambda a: jnp.zeros(a.shape, a.dtype), shapes)
    )


def kernel_call(body, outs, ins, args, grid=(1,), scratch=(), aliases=None, flops=0, vmem=14):
    moved = sum(a.size * a.dtype.itemsize for a in args)
    moved += sum(o.size * o.dtype.itemsize for o, _ in outs)
    return pl.pallas_call(
        body,
        grid=grid,
        in_specs=list(ins),
        out_specs=[spec for _, spec in outs],
        out_shape=[shape for shape, _ in outs],
        scratch_shapes=list(scratch),
        input_output_aliases=aliases or {},
        cost_estimate=pl.CostEstimate(flops=1024, bytes_accessed=1024, transcendentals=0),
        compiler_params=pltpu.CompilerParams(vmem_limit_bytes=vmem * 2**20),
    )(*args)


def shape(dims, dtype):
    return jax.ShapeDtypeStruct(dims, dtype)


def rows_spec(rows, cols, start=0):
    return pl.BlockSpec((rows, cols), lambda i: (i + start, 0))


def batch_spec(rows, cols, start=0):
    return pl.BlockSpec((1, rows, cols), lambda i: (i + start, 0, 0))


def once_spec(*dims):
    return pl.BlockSpec(dims, lambda i: (0,) * len(dims), pipeline_mode=pl.Buffered(1))


def whole_spec(*dims):
    return pl.BlockSpec(dims, lambda i: (0,) * len(dims))


ANY = pl.BlockSpec(memory_space=pl.ANY)
SMEM = pl.BlockSpec(memory_space=pltpu.SMEM)


def load_chunks(places, parts, target, sem, columns):
    copies, at = [], 0
    for part in parts:
        count, rows = part.shape[0], part.shape[1]
        for i in range(count):
            start = pl.multiple_of(places[at] * rows, 16)
            copies.append(
                pltpu.make_async_copy(part.at[i], target.at[pl.ds(start, rows), columns], sem)
            )
            at += 1
    return copies


def start_all(copies):
    for copy in copies:
        copy.start()


def wait_all(copies):
    for copy in copies:
        copy.wait()


def left_half():
    return lax.broadcasted_iota(jnp.int32, (1, LANES), 1) < HD


def wide(columns, pair):
    return jnp.where(
        left_half(), columns[:, 2 * pair : 2 * pair + 1], columns[:, 2 * pair + 1 : 2 * pair + 2]
    )


def one_half(values, side):
    keep = left_half() if side == 0 else jnp.logical_not(left_half())
    return jnp.where(keep, values, jnp.zeros_like(values))


def split(value, parts):
    found = []
    for _ in range(parts):
        low = value.astype(BF16)
        found.append(low)
        value = value - low.astype(F32)
    return found


def triangle(length, below):
    r = lax.broadcasted_iota(jnp.int32, (length, length), 0)
    c = lax.broadcasted_iota(jnp.int32, (length, length), 1)
    return jnp.where(r >= c if below else r <= c, 1.0, 0.0).astype(BF16)


def silu(v):
    return v * jax.nn.sigmoid(v)


def dsilu(v):
    s = jax.nn.sigmoid(v)
    return s * (1.0 + v * (1.0 - s))


def softplus(v):
    return jnp.maximum(v, 0.0) + jnp.log1p(jnp.exp(-jnp.abs(v)))


def at_index(me, pieces, index):
    count = len(pieces)
    found = pieces[0]
    for step in range(1, count):
        found = jnp.where(lax.rem(me - step + count, count) == index, pieces[step], found)
    return found


def rest_kernel(count, me, *refs):
    pieces, (dt_proj, gain, rest, conv_rows) = refs[:count], refs[count:]
    (rows, heads), own = dt_proj.shape, pieces[0].shape[1]
    ordered = [at_index(me[0], [p[...] for p in pieces], j) for j in range(count)]
    ordered = jnp.concatenate(ordered, axis=1)
    rest[:, : count * own] = ordered[:rows].astype(BF16)
    rest[:, count * own :] = jnp.zeros((rows, LANES), BF16)
    rest[:, count * own : count * own + heads] = dt_proj[...]
    rest[:, count * own + heads : count * own + heads + 1] = gain[...]
    conv_rows[...] = ordered[rows:]


def aux_kernel(seg_ref, aux, seg_row):
    blocks, length = seg_row.shape[0], seg_row.shape[2]
    for b in range(blocks):
        ids = seg_ref[b : b + 1]
        here = ids[:, GHOST:]
        rows = [ids[:, FIRST + k : FIRST + k + length] == here for k in range(KW)]
        rows += [here == here[:, length - 1 :], here == ids[:, GHOST - 1 : GHOST]]
        rows = [jnp.where(r, 1.0, 0.0) for r in rows] + [here.astype(F32)]
        rows += [jnp.zeros((LANES - len(rows), length), F32)]
        aux[b * length : (b + 1) * length] = jnp.concatenate(rows, axis=0).T
        seg_row[b] = jnp.broadcast_to(here.astype(F32), (8, length))


def conv_pair(source, weight, masks, length, columns):
    last = FIRST + KW - 1
    result = weight[KW : KW + 1, columns] + weight[KW - 1 : KW, columns] * (
        source[last : last + length, columns]
    )
    for tap in range(KW - 1):
        result = result + weight[tap : tap + 1, columns] * (
            source[FIRST + tap : FIRST + tap + length, columns] * masks[tap]
        )
    return result


def tap_masks(aux, length):
    return [jnp.broadcast_to(aux[:, k : k + 1], (length, LANES)) for k in range(KW - 1)]


def project_kernel(part_count, heads, *refs):
    places = refs[0]
    x_parts = refs[1 : 1 + part_count]
    b_parts = refs[1 + part_count : 1 + 2 * part_count]
    (tail, token, aux, conv_x, conv_bc, params, unit, x_ext, bc_ext, dt_raw, x_act, x_slope,
     bc_act, bc_slope, steps, local, chain, gain_row, weight, x_rows, b_rows, weighted,
     sem) = refs[1 + 2 * part_count :]
    length, inner = x_act.shape

    @pl.when(pl.program_id(0) == 0)
    def _():
        copies = load_chunks(places, x_parts, weight, sem, pl.ds(0, inner))
        copies += load_chunks(places, b_parts, weight, sem, pl.ds(inner, weight.shape[1] - inner))
        start_all(copies)
        wait_all(copies)
        turned = weight[:, inner + 2 * NS :].astype(F32).T
        gain_row[...] = jnp.broadcast_to(turned[heads : heads + 1], gain_row.shape)

    def scaled(v):
        scale = lax.rsqrt(jnp.mean(v * v, axis=-1, keepdims=True) + eps)
        return (v * scale * gain_row[0:1]).astype(BF16)

    def activate(v):
        sig = jax.nn.sigmoid(v)
        return (v * sig).astype(BF16), (sig * (1.0 + v * (1.0 - sig))).astype(BF16)

    unit[:GHOST] = scaled(tail[...].astype(F32))
    unit[GHOST:] = scaled(token[...].astype(F32))
    u = unit[...]
    rest = dot_nn(u, weight[:, inner:])
    bc_pre = rest[:, : 2 * NS].astype(BF16)
    bc_ext[...] = bc_pre
    b_rows[...] = bc_pre.astype(F32)
    raw = rest[GHOST:, 2 * NS :]
    dt_raw[...] = raw
    x_pre = dot_nn(u, weight[:, :inner]).astype(BF16)
    x_ext[...] = x_pre
    x_rows[...] = x_pre.astype(F32)
    masks = tap_masks(aux, length)
    for c in range(2):
        cols = slice(c * LANES, (c + 1) * LANES)
        act, slope = activate(conv_pair(b_rows, conv_bc, masks, length, cols))
        bc_act[:, cols] = act
        bc_slope[:, cols] = slope
    dt = softplus(raw + params[0:1])
    rate = -params[1:2] * dt
    lower = triangle(length, True)
    cum = sum(dot_nn(lower, part) for part in split(rate, 3))
    steps[:, :LANES] = dt
    steps[:, LANES:] = cum
    at_end = aux[:, AT_END : AT_END + 1]
    factor = dt * (at_end * jnp.exp(cum[length - 1 :] - cum))
    leave = aux[length - 1 :, AT_ENTRY : AT_ENTRY + 1] * jnp.exp(cum[length - 1 :])
    b_turned = bc_act[:, :NS].astype(F32).T.astype(BF16)
    for p in range(inner // LANES):
        cols = slice(p * LANES, (p + 1) * LANES)
        x, slope = activate(conv_pair(x_rows, conv_x, masks, length, cols))
        x_act[:, cols] = x
        x_slope[:, cols] = slope
        weighted[:, cols] = (x.astype(F32) * wide(factor, p)).astype(BF16)
        chain[0, :, cols] = jnp.broadcast_to(wide(leave, p), (8, LANES))
    local[0] = dot_nn(b_turned, weighted[...])


def pair_bias(aux, seg_row, flipped):
    length = aux.shape[0]
    r = lax.broadcasted_iota(jnp.int32, (length, length), 0)
    c = lax.broadcasted_iota(jnp.int32, (length, length), 1)
    seen = r <= c if flipped else r >= c
    same = aux[:, SEG : SEG + 1] == seg_row[0, 0:1]
    return jnp.where(jnp.logical_and(seen, same), 0.0, -1e30)


def intra_kernel(x_act, bc_act, steps, aux, seg_row, params, y_ref):
    dt, cum = steps[:, :LANES], steps[:, LANES:]
    cum_rows = cum.T
    bias = pair_bias(aux, seg_row, False)
    scores = dot_nt(bc_act[:, NS:], bc_act[:, :NS])
    skip = params[2:3]
    for p in range(x_act.shape[1] // LANES):
        cols = slice(p * LANES, (p + 1) * LANES)
        x = x_act[:, cols].astype(F32)
        x_dt = (x * wide(dt, p)).astype(BF16)
        total = wide(skip, p) * x
        for side in range(2):
            h = 2 * p + side
            falloff = jnp.exp(cum[:, h : h + 1] - cum_rows[h : h + 1] + bias)
            total = total + dot_nn((scores * falloff).astype(BF16), one_half(x_dt, side))
        y_ref[:, cols] = total.astype(BF16)


def order_kernel(part_count, places, *refs):
    parts, outs = refs[:part_count], refs[part_count:]
    step, low = pl.program_id(0), 0
    for part in parts:
        count = pl.num_programs(0) // part_count

        @pl.when(jnp.logical_and(step >= low, step < low + count))
        def _(part=part):
            at = 0
            for out in outs:
                out[...] = part[0, :, at : at + out.shape[1]]
                at += out.shape[1]

        low = low + count


def gated_kernel(y, bc_act, state, steps, aux, gate_z, d_gnorm, gains, ssd_ref, scaled, sums,
                 carried):
    length, inner = y.shape
    entry = aux[:, AT_ENTRY : AT_ENTRY + 1] * jnp.exp(steps[:, LANES:])
    carried[...] = dot_nn(bc_act[:, NS:], state[0])
    square = jnp.zeros((length, LANES), F32)
    along = jnp.zeros((length, LANES), F32)
    for p in range(inner // LANES):
        cols = slice(p * LANES, (p + 1) * LANES)
        ssd = y[:, cols].astype(F32) + wide(entry, p) * carried[:, cols]
        ssd_ref[:, cols] = ssd
        gated = ssd * silu(gate_z[GHOST:, cols].astype(F32))
        lifted = gated * gains[0:1, cols]
        scaled[:, cols] = lifted.astype(BF16)
        square = square + gated * gated
        along = along + d_gnorm[:, cols].astype(F32) * lifted
    lane = lax.broadcasted_iota(jnp.int32, (1, LANES), 1)
    both = jnp.where(
        lane == 0,
        jnp.sum(square, axis=1, keepdims=True),
        jnp.sum(along, axis=1, keepdims=True),
    )
    sums[0] = both.T[:8]


def branch_kernel(scaled, weight, *outs):
    length = outs[0].shape[0]
    found = dot_nt(scaled[...], weight[...]).astype(BF16)
    for b, out in enumerate(outs):
        out[...] = found[b * length : (b + 1) * length]


def norm_columns(sums):
    columns = jnp.concatenate([sums[0]] * (LANES // 8), axis=0).T
    scale = lax.rsqrt(columns[:, 0:1] / DI + eps)
    return scale, scale * scale * scale * columns[:, 1:2] / DI


def back_kernel(count, me, *refs):
    pieces = refs[:count]
    (ssd_ref, gate_z, d_gnorm, steps, aux, bc_act, gains, d_ssd, d_gate, g_norm, state_grad, scales,
     grad_gain, d_entry) = refs[count:]
    length, inner = ssd_ref.shape
    pieces = [p[...] for p in pieces]
    scale, inner_scale = norm_columns(sum(at_index(me[0], pieces, j) for j in range(count)))
    scales[...] = jnp.broadcast_to(scale, scales.shape)
    entry = aux[:, AT_ENTRY : AT_ENTRY + 1] * jnp.exp(steps[:, LANES:])
    c_turned = bc_act[:, NS:].astype(F32).T.astype(BF16)
    d_gate[:GHOST] = jnp.zeros((GHOST, inner), BF16)

    @pl.when(pl.program_id(0) == 0)
    def _():
        grad_gain[...] = jnp.zeros_like(grad_gain)

    for p in range(inner // LANES):
        cols = slice(p * LANES, (p + 1) * LANES)
        ssd = ssd_ref[:, cols]
        z, back = gate_z[GHOST:, cols].astype(F32), d_gnorm[:, cols].astype(F32)
        sig = jax.nn.sigmoid(z)
        act = z * sig
        gain = gains[0:1, cols]
        gated = ssd * act
        normed = gated * scale
        g_norm[:, cols] = (normed * gain).astype(BF16)
        grad_gain[0:1, cols] += jnp.sum(back * normed, axis=0, keepdims=True)
        d_gated = scale * (back * gain) - gated * inner_scale
        low = (d_gated * act).astype(BF16)
        d_ssd[:, cols] = low
        d_gate[GHOST:, cols] = (d_gated * ssd * (sig + act * (1.0 - sig))).astype(BF16)
        d_entry[:, cols] = (low.astype(F32) * wide(entry, p)).astype(BF16)
    state_grad[0] = dot_nn(c_turned, d_entry[...])


def intra_back_kernel(d_ssd, x_act, bc_act, steps, aux, seg_row, *refs):
    d_x_dt, d_bc = refs[-2:]
    dt, cum = steps[:, :LANES], steps[:, LANES:]
    length = cum.shape[0]
    cum_rows = cum.T
    bias = pair_bias(aux, seg_row, True)
    b_mat, c_mat = bc_act[:, :NS], bc_act[:, NS:]
    scores = dot_nt(b_mat, c_mat)
    d_scores = jnp.zeros((length, length), F32)
    for p in range(x_act.shape[1] // LANES):
        cols = slice(p * LANES, (p + 1) * LANES)
        x_dt = (x_act[:, cols].astype(F32) * wide(dt, p)).astype(BF16)
        d_out = d_ssd[:, cols]
        total = jnp.zeros((length, LANES), F32)
        for side in range(2):
            h = 2 * p + side
            falloff = jnp.exp(cum_rows[h : h + 1] - cum[:, h : h + 1] + bias)
            total = total + dot_nn((scores * falloff).astype(BF16), one_half(d_out, side))
            d_scores = d_scores + dot_nt(one_half(x_dt, side), d_out) * falloff
        d_x_dt[:, cols] = total.astype(BF16)
    d_bc[:, :NS] = dot_nn(d_scores.astype(BF16), c_mat)
    d_bc[:, NS:] = dot_nn(d_scores.T.astype(BF16), b_mat)


def conv_back(source, weight, masks, d_conv, columns, rows, taps):
    length = d_conv.shape[0]
    rows[:GHOST] = jnp.zeros((GHOST, LANES), F32)
    for tap in reversed(range(KW)):
        span = slice(FIRST + tap, FIRST + tap + length)
        part = d_conv if tap == KW - 1 else d_conv * masks[tap]
        taps[tap : tap + 1, columns] += jnp.sum(part * source[span, columns], axis=0, keepdims=True)
        moved = weight[tap : tap + 1, columns] * part
        rows[span] = moved if tap == KW - 1 else rows[span] + moved
    taps[KW : KW + 1, columns] += jnp.sum(d_conv, axis=0, keepdims=True)


def last_kernel(back, state, leaving, d_ssd, x_act, ssd_ref, bc_act, steps, dt_raw, aux, d_x_dt0,
                d_bc0, x_ext, bc_ext, x_slope, bc_slope, conv_x, conv_bc, params, *refs):
    (d_pre, x_grads, bc_grads, head_grads, x_rows, b_rows, rows, d_weighted, weighted,
     d_entry, out_high, out_low, in_high, in_low) = refs[-14:]
    length, inner = ssd_ref.shape
    dt, cum = steps[:, :LANES], steps[:, LANES:]
    end_decay = aux[:, AT_END : AT_END + 1] * jnp.exp(cum[length - 1 :] - cum)
    entry = aux[:, AT_ENTRY : AT_ENTRY + 1] * jnp.exp(cum)
    factor = dt * end_decay
    masks = tap_masks(aux, length)
    skip = params[2:3]
    x_rows[...] = x_ext[...].astype(F32)
    b_rows[...] = bc_ext[...].astype(F32)
    d_weighted[...] = dot_nn(bc_act[:, :NS], back[0])

    @pl.when(pl.program_id(0) == 0)
    def _():
        for ref in (x_grads, bc_grads, head_grads):
            ref[...] = jnp.zeros_like(ref)

    for p in range(inner // LANES):
        cols = slice(p * LANES, (p + 1) * LANES)
        x = x_act[:, cols].astype(F32)
        d_out = d_ssd[:, cols].astype(F32)
        skip_wide = wide(skip, p)
        d_x_dt = d_x_dt0[:, cols].astype(F32) + wide(end_decay, p) * d_weighted[:, cols]
        d_x = skip_wide * d_out + wide(dt, p) * d_x_dt
        weighted[:, cols] = (x * wide(factor, p)).astype(BF16)
        d_entry[:, cols] = (wide(entry, p) * d_out).astype(BF16)
        out_high[:, cols], out_low[:, cols] = split(
            d_out * (ssd_ref[:, cols] - skip_wide * x), 2
        )
        in_high[:, cols], in_low[:, cols] = split(x * d_x_dt, 2)
        x_grads[KW + 1 : KW + 2, cols] += jnp.sum(d_out * x, axis=0, keepdims=True)
        d_conv = d_x * x_slope[:, cols].astype(F32)
        conv_back(x_rows, conv_x, masks, d_conv, cols, rows, x_grads)
        d_pre[:, cols] = rows[...].astype(BF16)
    d_b = d_bc0[:, :NS] + dot_nt(weighted[...], back[0])
    d_c = d_bc0[:, NS:] + dot_nt(d_entry[...], state[0])
    for c, d_half in enumerate((d_b, d_c)):
        cols = slice(c * LANES, (c + 1) * LANES)
        d_conv = d_half * bc_slope[:, cols].astype(F32)
        conv_back(b_rows, conv_bc, masks, d_conv, cols, rows, bc_grads)
        d_pre[:, inner + c * LANES : inner + (c + 1) * LANES] = rows[...].astype(BF16)
    lane = lax.broadcasted_iota(jnp.int32, (inner, LANES), 1)
    first = lax.broadcasted_iota(jnp.int32, (inner, LANES), 0) - lane * HD
    pick = jnp.where(jnp.logical_and(first >= 0, first < HD), 1.0, 0.0).astype(BF16)
    out_dot = dot_nn(out_high[...], pick) + dot_nn(out_low[...], pick)
    in_dot = dot_nn(in_high[...], pick) + dot_nn(in_low[...], pick)
    ends = jnp.sum(back[0].astype(F32) * leaving[0], axis=0, keepdims=True)
    ends = split(jnp.broadcast_to(ends, (16, inner)), 2)
    last = sum(dot_nn(part, pick) for part in ends)
    d_cum = out_dot - dt * in_dot
    at_last = lax.broadcasted_iota(jnp.int32, (length, 1), 0) == length - 1
    d_cum = d_cum + jnp.where(at_last, last[0:1], 0.0)
    upper = triangle(length, False)
    d_rate = sum(dot_nn(upper, part) for part in split(d_cum, 3))
    d_dt = in_dot - params[1:2] * d_rate
    d_raw = d_dt * jax.nn.sigmoid(dt_raw[...] + params[0:1])
    head_grads[0:1] += jnp.sum(d_raw, axis=0, keepdims=True)
    head_grads[1:2] += jnp.sum(-dt * d_rate, axis=0, keepdims=True)
    d_pre[:GHOST, inner + 2 * NS :] = jnp.zeros((GHOST, LANES), BF16)
    d_pre[GHOST:, inner + 2 * NS :] = d_raw.astype(BF16)


def mains_kernel(blocks, d_unit, came, out):
    length, ext = out.shape[0] // blocks, d_unit.shape[0] // blocks
    for b in range(blocks):
        at, tail = b * length, (b + 1) * length - GHOST
        out[at:tail] = d_unit[b * ext + GHOST : b * ext + length]
        own = d_unit[b * ext + length : (b + 1) * ext].astype(F32)
        came_b = came[b * GHOST : (b + 1) * GHOST].astype(F32)
        out[tail : tail + GHOST] = (own + came_b).astype(BF16)


def copy_kernel(places, *refs):
    sources, out = refs[:-1], refs[-1]
    at = 0
    for source in sources:
        out[0, :, at : at + source.shape[1]] = source[...]
        at += source.shape[1]


def output_kernel(branch, tokens, scales, out):
    out[...] = (tokens[...].astype(F32) + scales[:, 0:1] * branch[...].astype(F32)).astype(BF16)


def token_grad_kernel(d_normed, tokens, cot, gain_row, out):
    d_unit = d_normed[...].astype(F32) * gain_row[0:1].astype(F32)
    tok = tokens[...].astype(F32)
    scale = lax.rsqrt(jnp.mean(tok * tok, axis=-1, keepdims=True) + eps)
    along = jnp.sum(d_unit * tok, axis=-1, keepdims=True) * (1.0 / D_MODEL)
    out[...] = cot[...].astype(F32) + scale * d_unit - tok * (scale * scale * scale * along)


def per_device(
    tokens,
    segment_ids,
    cotangent,
    in_gain,
    z_proj,
    x_proj,
    bc_proj,
    dt_proj,
    out_proj,
    conv_x,
    conv_x_bias,
    conv_bc,
    conv_bc_bias,
    dt_bias,
    decay_rate,
    skip_gain,
    out_gain,
):
    micro_count, row_count, length, width = tokens.shape
    blocks = micro_count * row_count
    token_count = blocks * length
    ext_len = length + GHOST
    ext_count = blocks * ext_len
    heads = skip_gain.shape[0]
    inner = conv_x.shape[1]
    bc_own = conv_bc.shape[1]
    bc_width = 2 * NS
    rest_width = bc_width + LANES
    pre_width = inner + rest_width
    shard_rows = in_gain.shape[0]
    seq_pos = lax.axis_index("seq")
    tensor_pos = lax.axis_index("tensor")
    seq_count = lax.axis_size("seq")
    tensor_count = lax.axis_size("tensor")
    me = tensor_pos.astype(jnp.int32)[None]
    at_edge = ((tensor_pos == 0) | (tensor_pos == tensor_count - 1)).astype(jnp.int32)[None]
    places = chunk_places()
    grid = (blocks,)
    halved = blocks // 2
    tile = 3 * LANES
    tiles = width // tile

    toks = tokens.reshape(blocks, length, width)
    cots = cotangent.reshape(blocks, length, width)
    flat_cot = cotangent.reshape(token_count, width)
    bc_pack = jnp.concatenate(
        [bc_proj.astype(F32), conv_bc, conv_bc_bias[None], jnp.zeros((3, bc_own), F32)]
    )
    bc_pieces = [bc_pack] + fetch_tensor(bc_pack)
    z_shard = jnp.concatenate([z_proj, out_proj.T], axis=1)
    x_came = z_came = x_proj
    if is_grid():
        x_came, z_came = cross_first(x_proj), cross_first(z_shard)
    tail = lax.ppermute(
        toks[:, length - GHOST :], "seq", [(i, i + 1) for i in range(seq_count - 1)]
    ).reshape(blocks * GHOST, width)
    rest_shard, conv_bc_rows = kernel_call(
        functools.partial(rest_kernel, tensor_count),
        [
            (shape((shard_rows, rest_width), BF16), whole_spec(shard_rows, rest_width)),
            (shape((8, bc_width), F32), whole_spec(8, bc_width)),
        ],
        [SMEM]
        + [whole_spec(shard_rows + 8, bc_own)] * tensor_count
        + [whole_spec(shard_rows, heads), whole_spec(shard_rows, 1)],
        (after(me, tail, x_came), *bc_pieces, dt_proj, in_gain[:, None]),
    )
    rest_came = cross_first(rest_shard) if is_grid() else None
    x_parts, x_far = gather_chunks(x_proj, x_came)
    b_parts, b_far = gather_chunks(rest_shard, rest_came, z_came, x_far)
    part_count = len(x_parts)
    conv_x_rows = jnp.concatenate([conv_x, conv_x_bias[None], jnp.zeros((3, inner), F32)])
    params = jnp.pad(
        jnp.stack([dt_bias, decay_rate, skip_gain]), ((0, 5), (0, LANES - heads))
    )
    gains = jnp.broadcast_to(out_gain[None], (8, inner))

    padded_ids = jnp.pad(
        segment_ids.reshape(blocks, -1), ((0, 0), (GHOST, 0)), constant_values=-1
    )
    seg_ext = lax.dynamic_slice_in_dim(padded_ids, seq_pos * length, ext_len, 1)
    aux, seg_row = kernel_call(
        aux_kernel,
        [
            (shape((token_count, LANES), F32), whole_spec(token_count, LANES)),
            (shape((blocks, 8, length), F32), whole_spec(blocks, 8, length)),
        ],
        [whole_spec(blocks, ext_len)],
        (seg_ext,),
    )

    aux_spec = rows_spec(length, LANES)
    steps_spec = rows_spec(length, 2 * LANES)
    inner_spec = rows_spec(length, inner)
    bc_spec = rows_spec(length, bc_width)
    state_spec = batch_spec(NS, inner)
    params_spec = whole_spec(8, LANES)
    (
        unit,
        x_ext,
        bc_ext,
        dt_raw,
        x_act,
        x_slope,
        bc_act,
        bc_slope,
        steps,
        local,
        chain,
        gain_row,
        w_pre,
    ) = kernel_call(
        functools.partial(project_kernel, part_count, heads),
        [
            (shape((ext_count, width), BF16), rows_spec(ext_len, width)),
            (shape((ext_count, inner), BF16), rows_spec(ext_len, inner)),
            (shape((ext_count, bc_width), BF16), rows_spec(ext_len, bc_width)),
            (shape((token_count, LANES), F32), aux_spec),
            (shape((token_count, inner), BF16), inner_spec),
            (shape((token_count, inner), BF16), inner_spec),
            (shape((token_count, bc_width), BF16), bc_spec),
            (shape((token_count, bc_width), BF16), bc_spec),
            (shape((token_count, 2 * LANES), F32), steps_spec),
            (shape((blocks, NS, inner), F32), state_spec),
            (shape((blocks, 8, inner), F32), batch_spec(8, inner)),
            (shape((8, width), F32), whole_spec(8, width)),
            (shape((width, pre_width), BF16), once_spec(width, pre_width)),
        ],
        [SMEM]
        + [ANY] * (2 * part_count)
        + [
            rows_spec(GHOST, width),
            rows_spec(length, width),
            aux_spec,
            whole_spec(8, inner),
            whole_spec(8, bc_width),
            params_spec,
        ],
        (
            places,
            *x_parts,
            *b_parts,
            tail,
            tokens.reshape(token_count, width),
            aux,
            conv_x_rows,
            conv_bc_rows,
            params,
        ),
        grid,
        scratch=[
            pltpu.VMEM((ext_len, inner), F32),
            pltpu.VMEM((ext_len, bc_width), F32),
            pltpu.VMEM((length, inner), BF16),
            pltpu.SemaphoreType.DMA,
        ],
        flops=2 * ext_count * width * (inner + rest_width),
        vmem=22,
    )
    (y_intra,) = kernel_call(
        intra_kernel,
        [(shape((token_count, inner), BF16), inner_spec)],
        [inner_spec, bc_spec, steps_spec, aux_spec, batch_spec(8, length), params_spec],
        (x_act, bc_act, steps, aux, seg_row, params),
        grid,
        flops=16 * token_count * length * inner,
    )
    z_parts, _ = gather_chunks(z_shard, z_came, b_far, late=chain)
    chunk_count = places.shape[0]
    each = chunk_count // part_count
    w_z, w_o = pl.pallas_call(
        functools.partial(order_kernel, part_count),
        grid_spec=pltpu.PrefetchScalarGridSpec(
            num_scalar_prefetch=1,
            grid=(chunk_count,),
            in_specs=[
                pl.BlockSpec(
                    (1, shard_rows, 2 * inner),
                    functools.partial(
                        lambda k, i, at: (jnp.clip(i - k * each, 0, each - 1), 0, 0), k
                    ),
                )
                for k in range(part_count)
            ],
            out_specs=[pl.BlockSpec((shard_rows, inner), lambda i, at: (at[i], 0))] * 2,
        ),
        out_shape=[shape((width, inner), BF16)] * 2,
        compiler_params=pltpu.CompilerParams(vmem_limit_bytes=8 * 2**20),
    )(places, *z_parts)
    gate_z = dot_nn(unit, w_z).astype(BF16)
    d_gnorm = dot_nn(flat_cot, w_o).astype(BF16)
    chain_row = chain[:, :1]
    state_in, state_out = state_scan(chain_row, local, False, (None, y_intra, w_z))
    ssd_out, scaled, own_sums = kernel_call(
        gated_kernel,
        [
            (shape((token_count, inner), F32), inner_spec),
            (shape((token_count, inner), BF16), inner_spec),
            (shape((blocks, 8, length), F32), batch_spec(8, length)),
        ],
        [
            inner_spec,
            bc_spec,
            state_spec,
            steps_spec,
            aux_spec,
            rows_spec(ext_len, inner),
            inner_spec,
            whole_spec(8, inner),
        ],
        (y_intra, bc_act, state_in, steps, aux, gate_z, d_gnorm, gains),
        grid,
        scratch=[pltpu.VMEM((length, inner), F32)],
        flops=2 * token_count * NS * inner,
    )
    sums = [own_sums] + fetch_tensor(own_sums)
    (branch_part,) = kernel_call(
        branch_kernel,
        [
            (shape((token_count, width), BF16), pl.BlockSpec((token_count, tile), lambda i: (0, i)))
        ],
        [once_spec(token_count, inner), rows_spec(tile, inner)],
        (scaled, w_o),
        (tiles,),
        flops=2 * token_count * width * inner,
    )

    branch = lax.psum(after(branch_part, *sums[1:]), "tensor")

    def backward():
        def half_call(body, start, filled, outs, shared, ins, args, scratch, flops, vmem=14):
            operands, specs, aliases = list(args), [spec(start) for spec in ins], {}
            if filled:
                aliases = {len(operands) + k: k for k in range(len(outs))}
                operands += filled
                specs += [ANY] * len(outs)
            made = kernel_call(
                body,
                [(o, spec(start)) for o, spec in outs] + list(shared),
                specs,
                operands,
                (halved,),
                scratch=scratch,
                aliases=aliases,
                flops=flops // 2,
                vmem=vmem,
            )
            return list(made[: len(outs)]), made[len(outs) :]

        def rows_from(rows, cols):
            return lambda start: rows_spec(rows, cols, start)

        def batch_from(rows, cols):
            return lambda start: batch_spec(rows, cols, start)

        def fixed(*dims):
            return lambda start: whole_spec(*dims)

        inner_from = rows_from(length, inner)
        bc_from = rows_from(length, bc_width)
        steps_from = rows_from(length, 2 * LANES)
        aux_from = rows_from(length, LANES)

        def intra_back(start, filled, token, d_ssd):
            return half_call(
                intra_back_kernel,
                start,
                filled,
                [
                    (shape((token_count, inner), BF16), inner_from),
                    (shape((token_count, bc_width), F32), bc_from),
                ],
                [],
                [inner_from, inner_from, bc_from, steps_from, aux_from, batch_from(8, length)],
                (d_ssd, x_act, bc_act, steps, aux, after(seg_row, *token)),
                [],
                32 * token_count * length * inner,
            )[0]

        def last(start, filled, token):
            return half_call(
                last_kernel,
                start,
                filled,
                [(shape((ext_count, pre_width), BF16), rows_from(ext_len, pre_width))],
                [
                    (shape((8, inner), F32), whole_spec(8, inner)),
                    (shape((8, bc_width), F32), whole_spec(8, bc_width)),
                    (shape((8, LANES), F32), params_spec),
                ],
                [
                    batch_from(NS, inner),
                    batch_from(NS, inner),
                    batch_from(NS, inner),
                    inner_from,
                    inner_from,
                    inner_from,
                    bc_from,
                    steps_from,
                    aux_from,
                    aux_from,
                    inner_from,
                    bc_from,
                    rows_from(ext_len, inner),
                    rows_from(ext_len, bc_width),
                    inner_from,
                    bc_from,
                    fixed(8, inner),
                    fixed(8, bc_width),
                    fixed(8, LANES),
                ],
                (
                    state_back,
                    state_in,
                    state_out,
                    d_ssd,
                    x_act,
                    ssd_out,
                    bc_act,
                    steps,
                    dt_raw,
                    aux,
                    d_x_dt,
                    d_bc,
                    x_ext,
                    bc_ext,
                    x_slope,
                    bc_slope,
                    conv_x_rows,
                    conv_bc_rows,
                    after(params, *token),
                ),
                [
                    pltpu.VMEM((ext_len, inner), F32),
                    pltpu.VMEM((ext_len, bc_width), F32),
                    pltpu.VMEM((ext_len, LANES), F32),
                    pltpu.VMEM((length, inner), F32),
                ]
                + [pltpu.VMEM((length, inner), BF16)] * 6,
                8 * token_count * NS * inner,
                22,
            )

        d_ssd, d_gate, g_norm, state_grad, scales, grad_out_gain = kernel_call(
            functools.partial(back_kernel, tensor_count),
            [
                (shape((token_count, inner), BF16), inner_spec),
                (shape((ext_count, inner), BF16), rows_spec(ext_len, inner)),
                (shape((token_count, inner), BF16), inner_spec),
                (shape((blocks, NS, inner), F32), state_spec),
                (shape((token_count, LANES), F32), aux_spec),
                (shape((8, inner), F32), whole_spec(8, inner)),
            ],
            [SMEM]
            + [batch_spec(8, length)] * tensor_count
            + [
                inner_spec,
                rows_spec(ext_len, inner),
                inner_spec,
                steps_spec,
                aux_spec,
                bc_spec,
                whole_spec(8, inner),
            ],
            (me, *sums, ssd_out, gate_z, d_gnorm, steps, aux, bc_act, gains),
            grid,
            scratch=[pltpu.VMEM((length, inner), BF16)],
            flops=2 * token_count * NS * inner,
        )

        first = intra_back(0, None, (), d_ssd)
        d_x_dt, d_bc = intra_back(halved, first, (), d_ssd)
        state_back, _ = state_scan(chain_row, state_grad, True, (first[1], d_bc))
        first_pre, first_grads = last(0, None, ())
        (d_pre,), last_grads = last(halved, first_pre, ())
        d_unit = (dot_nt(d_gate, w_z) + dot_nt(d_pre, w_pre)).astype(BF16)
        ghost = d_unit.reshape(blocks, ext_len, width)[:, :GHOST].reshape(blocks * GHOST, width)
        from_next = lax.ppermute(ghost, "seq", [(i + 1, i) for i in range(seq_count - 1)])
        (d_part,) = kernel_call(
            functools.partial(mains_kernel, blocks),
            [(shape((token_count, width), BF16), pl.BlockSpec((token_count, tile), lambda i: (0, i)))],
            [
                pl.BlockSpec((ext_count, tile), lambda i: (0, i)),
                pl.BlockSpec((blocks * GHOST, tile), lambda i: (0, i)),
            ],
            (d_unit, from_next),
            (tiles,),
        )
        return d_gate, d_pre, g_norm, scales, d_part, grad_out_gain, first_grads, last_grads

    d_gate, d_pre, g_norm, scales, d_part, grad_out_gain, first_grads, last_grads = in_turn(
        me, (branch_part, *sums), backward
    )
    d_normed = lax.psum(after(d_part, branch), "tensor")

    def weight_grad(*pairs):
        found = [
            lax.dot_general(
                left, right, (((0,), (0,)), ((), ())), preferred_element_type=F32
            ).astype(BF16)
            for left, right in pairs
        ]
        columns = sum(f.shape[1] for f in found)

        def chunks(low, high):
            return pl.pallas_call(
                copy_kernel,
                grid_spec=pltpu.PrefetchScalarGridSpec(
                    num_scalar_prefetch=1,
                    grid=(high - low,),
                    in_specs=[
                        pl.BlockSpec((shard_rows, f.shape[1]), lambda i, at: (at[i], 0))
                        for f in found
                    ],
                    out_specs=pl.BlockSpec((1, shard_rows, columns), lambda i, at: (i, 0, 0)),
                ),
                out_shape=shape((high - low, shard_rows, columns), BF16),
                compiler_params=pltpu.CompilerParams(vmem_limit_bytes=8 * 2**20),
            )(places[low:high], *found)

        if not is_grid():
            return (chunks(0, chunk_count),) * 2
        return chunks(4, 8), chunks(0, 4)

    small = jnp.concatenate(
        [
            first_grads[0] + last_grads[0],
            grad_out_gain,
            first_grads[1] + last_grads[1],
            first_grads[2] + last_grads[2],
        ],
        axis=1,
    )

    def closing():
        moved = weight_grad((unit, d_gate), (unit, d_pre), (flat_cot, g_norm))
        grads = sum_first(*sum_second(*sum_cores(*moved)))
        summed = small_sum(small, ("seq", "dp"))
        bc_part = grads[:, 2 * inner : 2 * inner + bc_width]
        bc_part = jnp.swapaxes(bc_part.reshape(shard_rows, tensor_count, bc_own), 0, 1)
        gain_part = (
            jnp.sum(grads[:, :inner] * z_proj.astype(F32), axis=1)
            + jnp.sum(grads[:, inner : 2 * inner] * x_proj.astype(F32), axis=1)
            + jnp.sum(grads[:, 2 * inner : inner + pre_width] * rest_shard.astype(F32), axis=1)
        )
        gain_part = jnp.pad(gain_part, (0, bc_width - shard_rows))[None]
        bc_sums = summed[: KW + 1, 2 * inner : 2 * inner + bc_width]
        bc_sums = jnp.concatenate([bc_sums, gain_part, jnp.zeros((2, bc_width), F32)])
        return (grads, summed, *sum_tensor(bc_part, bc_sums))

    grads, small, grad_bc, shared = in_turn(me, (branch,), closing)
    grad_z, grad_x = grads[:, :inner], grads[:, inner : 2 * inner]
    grad_dt = grads[:, 2 * inner + bc_width : 2 * inner + bc_width + heads]
    grad_out = grads[:, inner + pre_width :].T
    x_sums = small[:, :inner]
    head_sums = small[:, 2 * inner + bc_width :]
    step = length // 2
    wide_spec = rows_spec(step, width)
    flat_tokens = tokens.reshape(token_count, width)
    (output,) = kernel_call(
        output_kernel,
        [(shape((token_count, width), BF16), wide_spec)],
        [wide_spec, wide_spec, rows_spec(step, LANES)],
        (after(branch, grads), flat_tokens, scales),
        (token_count // step,),
    )
    (token_grad,) = kernel_call(
        token_grad_kernel,
        [(shape((token_count, width), F32), wide_spec)],
        [wide_spec, wide_spec, wide_spec, whole_spec(8, width)],
        (after(d_normed, output), flat_tokens, flat_cot, gain_row),
        (token_count // step,),
    )
    bc_mine = lax.dynamic_slice_in_dim(shared[: KW + 1], tensor_pos * bc_own, bc_own, 1)
    return (
        output.reshape(tokens.shape),
        token_grad.reshape(tokens.shape),
        shared[KW + 1, :shard_rows] / in_gain.astype(F32),
        grad_z,
        grad_x,
        grad_bc,
        grad_dt,
        grad_out,
        x_sums[:KW],
        x_sums[KW],
        bc_mine[:KW],
        bc_mine[KW],
        head_sums[0, :heads],
        head_sums[1, :heads],
        jnp.sum(x_sums[KW + 1].reshape(heads, HD), axis=1),
        small[0, inner : 2 * inner],
    )


def solution(mesh):
    in_specs = (
        P(None, "dp", "seq", None),
        P(None, "dp", None),
        P(None, "dp", "seq", None),
        P(("dp", "seq")),
        P(("dp", "seq"), "tensor"),
        P(("dp", "seq"), "tensor"),
        P(("dp", "seq"), "tensor"),
        P(("dp", "seq"), "tensor"),
        P("tensor", ("dp", "seq")),
        P(None, "tensor"),
        P("tensor"),
        P(None, "tensor"),
        P("tensor"),
        P("tensor"),
        P("tensor"),
        P("tensor"),
        P("tensor"),
    )
    out_specs = (
        P(None, "dp", "seq", None),
        P(None, "dp", "seq", None),
        P(("dp", "seq")),
        P(("dp", "seq"), "tensor"),
        P(("dp", "seq"), "tensor"),
        P(("dp", "seq"), "tensor"),
        P(("dp", "seq"), "tensor"),
        P("tensor", ("dp", "seq")),
        P(None, "tensor"),
        P("tensor"),
        P(None, "tensor"),
        P("tensor"),
        P("tensor"),
        P("tensor"),
        P("tensor"),
        P("tensor"),
    )
    return jax.shard_map(
        per_device, mesh=mesh, in_specs=in_specs, out_specs=out_specs, check_vma=False
    )
```

```python
import functools

import jax
import jax.numpy as jnp
from jax import lax
from jax.experimental import pallas as pl
from jax.experimental.pallas import tpu as pltpu
from jax.sharding import PartitionSpec as P

DI = 3072
D_MODEL = 1536
HD = 64
NS = 128
KW = 4
GHOST = 16
LANES = 128
FIRST = GHOST - KW + 1
AT_END, AT_ENTRY, SEG = KW, KW + 1, KW + 2

eps = 1e-05
F32 = jnp.float32
BF16 = jnp.bfloat16


def dot_nn(a, b):
    return lax.dot_general(a, b, (((1,), (0,)), ((), ())), preferred_element_type=F32)


def dot_nt(a, b):
    return lax.dot_general(a, b, (((1,), (1,)), ((), ())), preferred_element_type=F32)


def pair_route(mask, seq_mask):
    count = lax.axis_size("seq")
    route = []
    for x in range(lax.axis_size("dp")):
        for s in range(count):
            flip_x, flip_y = mask if s % 2 == 0 else seq_mask
            route.append((x * count + s, (x ^ flip_x) * count + (s ^ flip_y)))
    return route


ALONG_X, ALONG_Y = (1, 0), (0, 2)


def cross_first(value):
    return lax.ppermute(value, ("dp", "seq"), pair_route(ALONG_X, ALONG_Y))


def cross_second(value):
    return lax.ppermute(value, ("dp", "seq"), pair_route(ALONG_Y, ALONG_X))


def swap(value, axis, mask):
    return lax.ppermute(value, axis, [(i, i ^ mask) for i in range(lax.axis_size(axis))])


def is_grid():
    return lax.axis_size("dp") == 2 and lax.axis_size("seq") == 4


def chunk_places():
    if not is_grid():
        return jnp.arange(lax.axis_size("dp") * lax.axis_size("seq"), dtype=jnp.int32)
    x = lax.axis_index("dp")
    y = lax.axis_index("seq") // 2
    core = lax.axis_index("seq") % 2
    places = []
    for c in (core, 1 - core):
        for first, second in ((0, 0), (1, 0), (0, 1), (1, 1)):
            flip_x = jnp.where(c == 0, first, second)
            flip_y = jnp.where(c == 0, second, first)
            places.append((x ^ flip_x) * 4 + (y ^ flip_y) * 2 + c)
    return jnp.stack(places).astype(jnp.int32)


def gather_chunks(shard, came, *tokens, late=None):
    if not is_grid():
        every = lax.all_gather(shard, ("dp", "seq"), axis=0)
        return (every,), every
    two = after(jnp.stack([shard, came]), *tokens)
    far = cross_second(two)
    four = jnp.concatenate([two, far if late is None else after(far, late)])
    return (four, swap(four, "seq", 1)), far


def plus(kept, came):
    return kept.astype(F32) + came.astype(F32)


def sum_cores(theirs, mine):
    if not is_grid():
        total = lax.psum_scatter(
            mine.reshape((-1,) + mine.shape[2:]),
            ("dp", "seq"),
            scatter_dimension=0,
            tiled=True,
        ).astype(F32)
        return total, total
    came = swap(theirs, "seq", 1)
    return plus(mine[:2], came[:2]), plus(mine[2:], came[2:]).astype(BF16)


def sum_second(kept, away, token):
    if not is_grid():
        return kept, away
    came = after(cross_second(away), token)
    return plus(kept[0], came[0]), plus(kept[1], came[1]).astype(BF16)


def sum_first(kept, away, token):
    return plus(kept, after(cross_first(away), token)) if is_grid() else kept


def small_sum(value, axes):
    for axis in axes:
        mask = 1
        while mask < lax.axis_size(axis):
            value = value + swap(value, axis, mask)
            mask *= 2
    return value


def fetch_tensor(value):
    count = lax.axis_size("tensor")
    return [
        lax.ppermute(value, "tensor", [(i, (i + step) % count) for i in range(count)])
        for step in range(1, count)
    ]


def sum_tensor(pieces, shared, token):
    count = lax.axis_size("tensor")
    me = lax.axis_index("tensor")
    rows, width = pieces.shape[1:]
    flat = shared.reshape(-1, width)
    total = lax.dynamic_index_in_dim(pieces, me, 0, keepdims=False)
    every = [flat]
    for step in range(1, count):
        away = lax.dynamic_index_in_dim(pieces, (me + step) % count, 0, keepdims=False)
        route = [(i, (i + step) % count) for i in range(count)]
        came = after(lax.ppermute(jnp.concatenate([away, flat]), "tensor", route), token)
        total = total + came[:rows]
        every.append(came[rows:])
    order = (me - jnp.arange(count)) % count
    pick = (order[:, None] == jnp.arange(count)[None]).astype(F32)
    every = jnp.stack(every)
    found = 0.0
    for j in range(count):
        found = found + jnp.sum(pick[j][:, None, None] * every, axis=0)
    return total, found.reshape(shared.shape)


def low_sum(kept, came):
    return plus(kept, came).astype(BF16)


def hop_in(value):
    return lax.ppermute(value, "tensor", [(0, 1), (3, 2)])


def hop_across(value):
    return lax.ppermute(value, "tensor", [(1, 2), (2, 1)])


def hop_out(value):
    return lax.ppermute(value, "tensor", [(1, 0), (2, 3)])


def state_scan(decay, local, backward, tokens=()):
    count = lax.axis_size("seq")
    state = jnp.zeros_like(local)
    leaving = local
    for hop in range(count - 1):
        pair = (count - 1 - hop, count - 2 - hop) if backward else (hop, hop + 1)
        came = lax.ppermute(leaving.astype(BF16), "seq", [pair])
        if hop < len(tokens):
            came = after(came, *tokens[hop])
        state = state + came.astype(F32)
        leaving = decay * state + local
    return state.astype(BF16), leaving


def after(value, *tokens):
    return lax.optimization_barrier((value,) + tokens)[0]


def in_turn(me, tokens, work):
    turn = after(me, *tokens)[0] >= 0
    shapes = jax.eval_shape(work)
    return lax.cond(
        turn, work, lambda: jax.tree.map(lambda a: jnp.zeros(a.shape, a.dtype), shapes)
    )


def kernel_call(body, outs, ins, args, grid=(1,), scratch=(), aliases=None, flops=0, vmem=14):
    moved = sum(a.size * a.dtype.itemsize for a in args)
    moved += sum(o.size * o.dtype.itemsize for o, _ in outs)
    return pl.pallas_call(
        body,
        grid=grid,
        in_specs=list(ins),
        out_specs=[spec for _, spec in outs],
        out_shape=[shape for shape, _ in outs],
        scratch_shapes=list(scratch),
        input_output_aliases=aliases or {},
        cost_estimate=pl.CostEstimate(flops=1024, bytes_accessed=1024, transcendentals=0),
        compiler_params=pltpu.CompilerParams(vmem_limit_bytes=vmem * 2**20),
    )(*args)


def shape(dims, dtype):
    return jax.ShapeDtypeStruct(dims, dtype)


def rows_spec(rows, cols, start=0):
    return pl.BlockSpec((rows, cols), lambda i: (i + start, 0))


def batch_spec(rows, cols, start=0):
    return pl.BlockSpec((1, rows, cols), lambda i: (i + start, 0, 0))


def once_spec(*dims):
    return pl.BlockSpec(dims, lambda i: (0,) * len(dims), pipeline_mode=pl.Buffered(1))


def whole_spec(*dims):
    return pl.BlockSpec(dims, lambda i: (0,) * len(dims))


ANY = pl.BlockSpec(memory_space=pl.ANY)
SMEM = pl.BlockSpec(memory_space=pltpu.SMEM)


def load_chunks(places, parts, target, sem, columns):
    copies, at = [], 0
    for part in parts:
        count, rows = part.shape[0], part.shape[1]
        for i in range(count):
            start = pl.multiple_of(places[at] * rows, 16)
            copies.append(
                pltpu.make_async_copy(part.at[i], target.at[pl.ds(start, rows), columns], sem)
            )
            at += 1
    return copies


def start_all(copies):
    for copy in copies:
        copy.start()


def wait_all(copies):
    for copy in copies:
        copy.wait()


def left_half():
    return lax.broadcasted_iota(jnp.int32, (1, LANES), 1) < HD


def wide(columns, pair):
    return jnp.where(
        left_half(), columns[:, 2 * pair : 2 * pair + 1], columns[:, 2 * pair + 1 : 2 * pair + 2]
    )


def one_half(values, side):
    keep = left_half() if side == 0 else jnp.logical_not(left_half())
    return jnp.where(keep, values, jnp.zeros_like(values))


def split(value, parts):
    found = []
    for _ in range(parts):
        low = value.astype(BF16)
        found.append(low)
        value = value - low.astype(F32)
    return found


def triangle(length, below):
    r = lax.broadcasted_iota(jnp.int32, (length, length), 0)
    c = lax.broadcasted_iota(jnp.int32, (length, length), 1)
    return jnp.where(r >= c if below else r <= c, 1.0, 0.0).astype(BF16)


def silu(v):
    return v * jax.nn.sigmoid(v)


def dsilu(v):
    s = jax.nn.sigmoid(v)
    return s * (1.0 + v * (1.0 - s))


def softplus(v):
    return jnp.maximum(v, 0.0) + jnp.log1p(jnp.exp(-jnp.abs(v)))


def at_index(me, pieces, index):
    count = len(pieces)
    found = pieces[0]
    for step in range(1, count):
        found = jnp.where(lax.rem(me - step + count, count) == index, pieces[step], found)
    return found


def rest_kernel(count, me, *refs):
    pieces, (dt_proj, gain, rest, conv_rows) = refs[:count], refs[count:]
    (rows, heads), own = dt_proj.shape, pieces[0].shape[1]
    ordered = [at_index(me[0], [p[...] for p in pieces], j) for j in range(count)]
    ordered = jnp.concatenate(ordered, axis=1)
    rest[:, : count * own] = ordered[:rows].astype(BF16)
    rest[:, count * own :] = jnp.zeros((rows, LANES), BF16)
    rest[:, count * own : count * own + heads] = dt_proj[...]
    rest[:, count * own + heads : count * own + heads + 1] = gain[...]
    conv_rows[...] = ordered[rows:]


def aux_kernel(seg_ref, aux, seg_row):
    blocks, length = seg_row.shape[0], seg_row.shape[2]
    for b in range(blocks):
        ids = seg_ref[b : b + 1]
        here = ids[:, GHOST:]
        rows = [ids[:, FIRST + k : FIRST + k + length] == here for k in range(KW)]
        rows += [here == here[:, length - 1 :], here == ids[:, GHOST - 1 : GHOST]]
        rows = [jnp.where(r, 1.0, 0.0) for r in rows] + [here.astype(F32)]
        rows += [jnp.zeros((LANES - len(rows), length), F32)]
        aux[b * length : (b + 1) * length] = jnp.concatenate(rows, axis=0).T
        seg_row[b] = jnp.broadcast_to(here.astype(F32), (8, length))


def conv_pair(source, weight, masks, length, columns):
    last = FIRST + KW - 1
    result = weight[KW : KW + 1, columns] + weight[KW - 1 : KW, columns] * (
        source[last : last + length, columns]
    )
    for tap in range(KW - 1):
        result = result + weight[tap : tap + 1, columns] * (
            source[FIRST + tap : FIRST + tap + length, columns] * masks[tap]
        )
    return result


def tap_masks(aux, length):
    return [jnp.broadcast_to(aux[:, k : k + 1], (length, LANES)) for k in range(KW - 1)]


def project_kernel(part_count, heads, *refs):
    places = refs[0]
    x_parts = refs[1 : 1 + part_count]
    b_parts = refs[1 + part_count : 1 + 2 * part_count]
    (tail, token, aux, conv_x, conv_bc, params, unit, x_ext, bc_ext, dt_raw, x_act, x_slope,
     bc_act, bc_slope, steps, local, chain, gain_row, weight, x_rows, b_rows, weighted,
     sem) = refs[1 + 2 * part_count :]
    length, inner = x_act.shape

    @pl.when(pl.program_id(0) == 0)
    def _():
        copies = load_chunks(places, x_parts, weight, sem, pl.ds(0, inner))
        copies += load_chunks(places, b_parts, weight, sem, pl.ds(inner, weight.shape[1] - inner))
        start_all(copies)
        wait_all(copies)
        turned = weight[:, inner + 2 * NS :].astype(F32).T
        gain_row[...] = jnp.broadcast_to(turned[heads : heads + 1], gain_row.shape)

    def scaled(v):
        scale = lax.rsqrt(jnp.mean(v * v, axis=-1, keepdims=True) + eps)
        return (v * scale * gain_row[0:1]).astype(BF16)

    def activate(v):
        sig = jax.nn.sigmoid(v)
        return (v * sig).astype(BF16), (sig * (1.0 + v * (1.0 - sig))).astype(BF16)

    unit[:GHOST] = scaled(tail[...].astype(F32))
    unit[GHOST:] = scaled(token[...].astype(F32))
    u = unit[...]
    rest = dot_nn(u, weight[:, inner:])
    bc_pre = rest[:, : 2 * NS].astype(BF16)
    bc_ext[...] = bc_pre
    b_rows[...] = bc_pre.astype(F32)
    raw = rest[GHOST:, 2 * NS :]
    dt_raw[...] = raw
    x_pre = dot_nn(u, weight[:, :inner]).astype(BF16)
    x_ext[...] = x_pre
    x_rows[...] = x_pre.astype(F32)
    masks = tap_masks(aux, length)
    for c in range(2):
        cols = slice(c * LANES, (c + 1) * LANES)
        act, slope = activate(conv_pair(b_rows, conv_bc, masks, length, cols))
        bc_act[:, cols] = act
        bc_slope[:, cols] = slope
    dt = softplus(raw + params[0:1])
    rate = -params[1:2] * dt
    lower = triangle(length, True)
    cum = sum(dot_nn(lower, part) for part in split(rate, 3))
    steps[:, :LANES] = dt
    steps[:, LANES:] = cum
    at_end = aux[:, AT_END : AT_END + 1]
    factor = dt * (at_end * jnp.exp(cum[length - 1 :] - cum))
    leave = aux[length - 1 :, AT_ENTRY : AT_ENTRY + 1] * jnp.exp(cum[length - 1 :])
    b_turned = bc_act[:, :NS].astype(F32).T.astype(BF16)
    for p in range(inner // LANES):
        cols = slice(p * LANES, (p + 1) * LANES)
        x, slope = activate(conv_pair(x_rows, conv_x, masks, length, cols))
        x_act[:, cols] = x
        x_slope[:, cols] = slope
        weighted[:, cols] = (x.astype(F32) * wide(factor, p)).astype(BF16)
        chain[0, :, cols] = jnp.broadcast_to(wide(leave, p), (8, LANES))
    local[0] = dot_nn(b_turned, weighted[...])


def pair_bias(aux, seg_row, flipped):
    length = aux.shape[0]
    r = lax.broadcasted_iota(jnp.int32, (length, length), 0)
    c = lax.broadcasted_iota(jnp.int32, (length, length), 1)
    seen = r <= c if flipped else r >= c
    same = aux[:, SEG : SEG + 1] == seg_row[0, 0:1]
    return jnp.where(jnp.logical_and(seen, same), 0.0, -1e30)


def intra_kernel(x_act, bc_act, steps, aux, seg_row, params, y_ref):
    dt, cum = steps[:, :LANES], steps[:, LANES:]
    cum_rows = cum.T
    bias = pair_bias(aux, seg_row, False)
    scores = dot_nt(bc_act[:, NS:], bc_act[:, :NS])
    skip = params[2:3]
    for p in range(x_act.shape[1] // LANES):
        cols = slice(p * LANES, (p + 1) * LANES)
        x = x_act[:, cols].astype(F32)
        x_dt = (x * wide(dt, p)).astype(BF16)
        total = wide(skip, p) * x
        for side in range(2):
            h = 2 * p + side
            falloff = jnp.exp(cum[:, h : h + 1] - cum_rows[h : h + 1] + bias)
            total = total + dot_nn((scores * falloff).astype(BF16), one_half(x_dt, side))
        y_ref[:, cols] = total.astype(BF16)


def order_kernel(part_count, places, *refs):
    parts, outs = refs[:part_count], refs[part_count:]
    step, low = pl.program_id(0), 0
    for part in parts:
        count = pl.num_programs(0) // part_count

        @pl.when(jnp.logical_and(step >= low, step < low + count))
        def _(part=part):
            at = 0
            for out in outs:
                out[...] = part[0, :, at : at + out.shape[1]]
                at += out.shape[1]

        low = low + count


def gated_kernel(y, bc_act, state, steps, aux, gate_z, d_gnorm, gains, ssd_ref, scaled, sums,
                 carried):
    length, inner = y.shape
    entry = aux[:, AT_ENTRY : AT_ENTRY + 1] * jnp.exp(steps[:, LANES:])
    carried[...] = dot_nn(bc_act[:, NS:], state[0])
    square = jnp.zeros((length, LANES), F32)
    along = jnp.zeros((length, LANES), F32)
    for p in range(inner // LANES):
        cols = slice(p * LANES, (p + 1) * LANES)
        ssd = y[:, cols].astype(F32) + wide(entry, p) * carried[:, cols]
        ssd_ref[:, cols] = ssd
        gated = ssd * silu(gate_z[GHOST:, cols].astype(F32))
        lifted = gated * gains[0:1, cols]
        scaled[:, cols] = lifted.astype(BF16)
        square = square + gated * gated
        along = along + d_gnorm[:, cols].astype(F32) * lifted
    lane = lax.broadcasted_iota(jnp.int32, (1, LANES), 1)
    both = jnp.where(
        lane == 0,
        jnp.sum(square, axis=1, keepdims=True),
        jnp.sum(along, axis=1, keepdims=True),
    )
    sums[0] = both.T[:8]


def branch_kernel(scaled, weight, *outs):
    length = outs[0].shape[0]
    found = dot_nt(scaled[...], weight[...]).astype(BF16)
    for b, out in enumerate(outs):
        out[...] = found[b * length : (b + 1) * length]


def norm_columns(sums):
    columns = jnp.concatenate([sums[0]] * (LANES // 8), axis=0).T
    scale = lax.rsqrt(columns[:, 0:1] / DI + eps)
    return scale, scale * scale * scale * columns[:, 1:2] / DI


def back_kernel(count, me, *refs):
    pieces = refs[:count]
    (ssd_ref, gate_z, d_gnorm, steps, aux, bc_act, gains, d_ssd, d_gate, g_norm, state_grad, scales,
     grad_gain, d_entry) = refs[count:]
    length, inner = ssd_ref.shape
    pieces = [p[...] for p in pieces]
    scale, inner_scale = norm_columns(sum(at_index(me[0], pieces, j) for j in range(count)))
    scales[...] = jnp.broadcast_to(scale, scales.shape)
    entry = aux[:, AT_ENTRY : AT_ENTRY + 1] * jnp.exp(steps[:, LANES:])
    c_turned = bc_act[:, NS:].astype(F32).T.astype(BF16)
    d_gate[:GHOST] = jnp.zeros((GHOST, inner), BF16)

    @pl.when(pl.program_id(0) == 0)
    def _():
        grad_gain[...] = jnp.zeros_like(grad_gain)

    for p in range(inner // LANES):
        cols = slice(p * LANES, (p + 1) * LANES)
        ssd = ssd_ref[:, cols]
        z, back = gate_z[GHOST:, cols].astype(F32), d_gnorm[:, cols].astype(F32)
        sig = jax.nn.sigmoid(z)
        act = z * sig
        gain = gains[0:1, cols]
        gated = ssd * act
        normed = gated * scale
        g_norm[:, cols] = (normed * gain).astype(BF16)
        grad_gain[0:1, cols] += jnp.sum(back * normed, axis=0, keepdims=True)
        d_gated = scale * (back * gain) - gated * inner_scale
        low = (d_gated * act).astype(BF16)
        d_ssd[:, cols] = low
        d_gate[GHOST:, cols] = (d_gated * ssd * (sig + act * (1.0 - sig))).astype(BF16)
        d_entry[:, cols] = (low.astype(F32) * wide(entry, p)).astype(BF16)
    state_grad[0] = dot_nn(c_turned, d_entry[...])


def intra_back_kernel(d_ssd, x_act, bc_act, steps, aux, seg_row, *refs):
    d_x_dt, d_bc = refs[-2:]
    dt, cum = steps[:, :LANES], steps[:, LANES:]
    length = cum.shape[0]
    cum_rows = cum.T
    bias = pair_bias(aux, seg_row, True)
    b_mat, c_mat = bc_act[:, :NS], bc_act[:, NS:]
    scores = dot_nt(b_mat, c_mat)
    d_scores = jnp.zeros((length, length), F32)
    for p in range(x_act.shape[1] // LANES):
        cols = slice(p * LANES, (p + 1) * LANES)
        x_dt = (x_act[:, cols].astype(F32) * wide(dt, p)).astype(BF16)
        d_out = d_ssd[:, cols]
        total = jnp.zeros((length, LANES), F32)
        for side in range(2):
            h = 2 * p + side
            falloff = jnp.exp(cum_rows[h : h + 1] - cum[:, h : h + 1] + bias)
            total = total + dot_nn((scores * falloff).astype(BF16), one_half(d_out, side))
            d_scores = d_scores + dot_nt(one_half(x_dt, side), d_out) * falloff
        d_x_dt[:, cols] = total.astype(BF16)
    d_bc[:, :NS] = dot_nn(d_scores.astype(BF16), c_mat)
    d_bc[:, NS:] = dot_nn(d_scores.T.astype(BF16), b_mat)


def conv_back(source, weight, masks, d_conv, columns, rows, taps):
    length = d_conv.shape[0]
    rows[:GHOST] = jnp.zeros((GHOST, LANES), F32)
    for tap in reversed(range(KW)):
        span = slice(FIRST + tap, FIRST + tap + length)
        part = d_conv if tap == KW - 1 else d_conv * masks[tap]
        taps[tap : tap + 1, columns] += jnp.sum(part * source[span, columns], axis=0, keepdims=True)
        moved = weight[tap : tap + 1, columns] * part
        rows[span] = moved if tap == KW - 1 else rows[span] + moved
    taps[KW : KW + 1, columns] += jnp.sum(d_conv, axis=0, keepdims=True)


def last_kernel(back, state, leaving, d_ssd, x_act, ssd_ref, bc_act, steps, dt_raw, aux, d_x_dt0,
                d_bc0, x_ext, bc_ext, x_slope, bc_slope, conv_x, conv_bc, params, *refs):
    (d_pre, x_grads, bc_grads, head_grads, x_rows, b_rows, rows, d_weighted, weighted,
     d_entry, out_high, out_low, in_high, in_low) = refs[-14:]
    length, inner = ssd_ref.shape
    dt, cum = steps[:, :LANES], steps[:, LANES:]
    end_decay = aux[:, AT_END : AT_END + 1] * jnp.exp(cum[length - 1 :] - cum)
    entry = aux[:, AT_ENTRY : AT_ENTRY + 1] * jnp.exp(cum)
    factor = dt * end_decay
    masks = tap_masks(aux, length)
    skip = params[2:3]
    x_rows[...] = x_ext[...].astype(F32)
    b_rows[...] = bc_ext[...].astype(F32)
    d_weighted[...] = dot_nn(bc_act[:, :NS], back[0])

    @pl.when(pl.program_id(0) == 0)
    def _():
        for ref in (x_grads, bc_grads, head_grads):
            ref[...] = jnp.zeros_like(ref)

    for p in range(inner // LANES):
        cols = slice(p * LANES, (p + 1) * LANES)
        x = x_act[:, cols].astype(F32)
        d_out = d_ssd[:, cols].astype(F32)
        skip_wide = wide(skip, p)
        d_x_dt = d_x_dt0[:, cols].astype(F32) + wide(end_decay, p) * d_weighted[:, cols]
        d_x = skip_wide * d_out + wide(dt, p) * d_x_dt
        weighted[:, cols] = (x * wide(factor, p)).astype(BF16)
        d_entry[:, cols] = (wide(entry, p) * d_out).astype(BF16)
        out_high[:, cols], out_low[:, cols] = split(
            d_out * (ssd_ref[:, cols] - skip_wide * x), 2
        )
        in_high[:, cols], in_low[:, cols] = split(x * d_x_dt, 2)
        x_grads[KW + 1 : KW + 2, cols] += jnp.sum(d_out * x, axis=0, keepdims=True)
        d_conv = d_x * x_slope[:, cols].astype(F32)
        conv_back(x_rows, conv_x, masks, d_conv, cols, rows, x_grads)
        d_pre[:, cols] = rows[...].astype(BF16)
    d_b = d_bc0[:, :NS] + dot_nt(weighted[...], back[0])
    d_c = d_bc0[:, NS:] + dot_nt(d_entry[...], state[0])
    for c, d_half in enumerate((d_b, d_c)):
        cols = slice(c * LANES, (c + 1) * LANES)
        d_conv = d_half * bc_slope[:, cols].astype(F32)
        conv_back(b_rows, conv_bc, masks, d_conv, cols, rows, bc_grads)
        d_pre[:, inner + c * LANES : inner + (c + 1) * LANES] = rows[...].astype(BF16)
    lane = lax.broadcasted_iota(jnp.int32, (inner, LANES), 1)
    first = lax.broadcasted_iota(jnp.int32, (inner, LANES), 0) - lane * HD
    pick = jnp.where(jnp.logical_and(first >= 0, first < HD), 1.0, 0.0).astype(BF16)
    out_dot = dot_nn(out_high[...], pick) + dot_nn(out_low[...], pick)
    in_dot = dot_nn(in_high[...], pick) + dot_nn(in_low[...], pick)
    ends = jnp.sum(back[0].astype(F32) * leaving[0], axis=0, keepdims=True)
    ends = split(jnp.broadcast_to(ends, (16, inner)), 2)
    last = sum(dot_nn(part, pick) for part in ends)
    d_cum = out_dot - dt * in_dot
    at_last = lax.broadcasted_iota(jnp.int32, (length, 1), 0) == length - 1
    d_cum = d_cum + jnp.where(at_last, last[0:1], 0.0)
    upper = triangle(length, False)
    d_rate = sum(dot_nn(upper, part) for part in split(d_cum, 3))
    d_dt = in_dot - params[1:2] * d_rate
    d_raw = d_dt * jax.nn.sigmoid(dt_raw[...] + params[0:1])
    head_grads[0:1] += jnp.sum(d_raw, axis=0, keepdims=True)
    head_grads[1:2] += jnp.sum(-dt * d_rate, axis=0, keepdims=True)
    d_pre[:GHOST, inner + 2 * NS :] = jnp.zeros((GHOST, LANES), BF16)
    d_pre[GHOST:, inner + 2 * NS :] = d_raw.astype(BF16)


def mains_kernel(d_unit, came, *outs):
    length, ext = outs[0].shape[0], d_unit.shape[0] // len(outs)
    for b, out in enumerate(outs):
        out[: length - GHOST] = d_unit[b * ext + GHOST : b * ext + length]
        tail = d_unit[b * ext + length : (b + 1) * ext].astype(F32)
        out[length - GHOST :] = (tail + came[b * GHOST : (b + 1) * GHOST].astype(F32)).astype(BF16)


def copy_kernel(places, *refs):
    sources, out = refs[:-1], refs[-1]
    at = 0
    for source in sources:
        out[0, :, at : at + source.shape[1]] = source[...]
        at += source.shape[1]


def output_kernel(branch, tokens, scales, out):
    out[...] = (tokens[...].astype(F32) + scales[:, 0:1] * branch[...].astype(F32)).astype(BF16)


def token_grad_kernel(at_edge, total, back, tokens, cot, gain_row, *refs):
    out = refs[-1]
    d_unit = jnp.where(at_edge[0] == 1, back[...].astype(F32), total[...].astype(F32))
    d_unit = d_unit * gain_row[0:1].astype(F32)
    tok = tokens[...].astype(F32)
    scale = lax.rsqrt(jnp.mean(tok * tok, axis=-1, keepdims=True) + eps)
    along = jnp.sum(d_unit * tok, axis=-1, keepdims=True) * (1.0 / D_MODEL)
    out[...] = cot[...].astype(F32) + scale * d_unit - tok * (scale * scale * scale * along)


def per_device(
    tokens,
    segment_ids,
    cotangent,
    in_gain,
    z_proj,
    x_proj,
    bc_proj,
    dt_proj,
    out_proj,
    conv_x,
    conv_x_bias,
    conv_bc,
    conv_bc_bias,
    dt_bias,
    decay_rate,
    skip_gain,
    out_gain,
):
    micro_count, row_count, length, width = tokens.shape
    blocks = micro_count * row_count
    token_count = blocks * length
    ext_len = length + GHOST
    ext_count = blocks * ext_len
    heads = skip_gain.shape[0]
    inner = conv_x.shape[1]
    bc_own = conv_bc.shape[1]
    bc_width = 2 * NS
    rest_width = bc_width + LANES
    pre_width = inner + rest_width
    shard_rows = in_gain.shape[0]
    seq_pos = lax.axis_index("seq")
    tensor_pos = lax.axis_index("tensor")
    seq_count = lax.axis_size("seq")
    tensor_count = lax.axis_size("tensor")
    me = tensor_pos.astype(jnp.int32)[None]
    at_edge = ((tensor_pos == 0) | (tensor_pos == tensor_count - 1)).astype(jnp.int32)[None]
    places = chunk_places()
    grid = (blocks,)
    halved = blocks // 2
    tile = 3 * LANES
    tiles = width // tile

    toks = tokens.reshape(blocks, length, width)
    cots = cotangent.reshape(blocks, length, width)
    flat_cot = cotangent.reshape(token_count, width)
    bc_pack = jnp.concatenate(
        [bc_proj.astype(F32), conv_bc, conv_bc_bias[None], jnp.zeros((3, bc_own), F32)]
    )
    bc_pieces = [bc_pack] + fetch_tensor(bc_pack)
    z_shard = jnp.concatenate([z_proj, out_proj.T], axis=1)
    x_came = z_came = x_proj
    if is_grid():
        x_came, z_came = cross_first(x_proj), cross_first(z_shard)
    tail = lax.ppermute(
        toks[:, length - GHOST :], "seq", [(i, i + 1) for i in range(seq_count - 1)]
    ).reshape(blocks * GHOST, width)
    rest_shard, conv_bc_rows = kernel_call(
        functools.partial(rest_kernel, tensor_count),
        [
            (shape((shard_rows, rest_width), BF16), whole_spec(shard_rows, rest_width)),
            (shape((8, bc_width), F32), whole_spec(8, bc_width)),
        ],
        [SMEM]
        + [whole_spec(shard_rows + 8, bc_own)] * tensor_count
        + [whole_spec(shard_rows, heads), whole_spec(shard_rows, 1)],
        (after(me, tail, x_came, z_came), *bc_pieces, dt_proj, in_gain[:, None]),
    )
    rest_came = cross_first(rest_shard) if is_grid() else None
    x_parts, x_far = gather_chunks(x_proj, x_came, rest_shard)
    b_parts, b_far = gather_chunks(rest_shard, rest_came, z_came, x_far)
    part_count = len(x_parts)
    conv_x_rows = jnp.concatenate([conv_x, conv_x_bias[None], jnp.zeros((3, inner), F32)])
    params = jnp.pad(
        jnp.stack([dt_bias, decay_rate, skip_gain]), ((0, 5), (0, LANES - heads))
    )
    gains = jnp.broadcast_to(out_gain[None], (8, inner))

    padded_ids = jnp.pad(
        segment_ids.reshape(blocks, -1), ((0, 0), (GHOST, 0)), constant_values=-1
    )
    seg_ext = lax.dynamic_slice_in_dim(padded_ids, seq_pos * length, ext_len, 1)
    aux, seg_row = kernel_call(
        aux_kernel,
        [
            (shape((token_count, LANES), F32), whole_spec(token_count, LANES)),
            (shape((blocks, 8, length), F32), whole_spec(blocks, 8, length)),
        ],
        [whole_spec(blocks, ext_len)],
        (seg_ext,),
    )

    aux_spec = rows_spec(length, LANES)
    steps_spec = rows_spec(length, 2 * LANES)
    inner_spec = rows_spec(length, inner)
    bc_spec = rows_spec(length, bc_width)
    state_spec = batch_spec(NS, inner)
    params_spec = whole_spec(8, LANES)
    (
        unit,
        x_ext,
        bc_ext,
        dt_raw,
        x_act,
        x_slope,
        bc_act,
        bc_slope,
        steps,
        local,
        chain,
        gain_row,
        w_pre,
    ) = kernel_call(
        functools.partial(project_kernel, part_count, heads),
        [
            (shape((ext_count, width), BF16), rows_spec(ext_len, width)),
            (shape((ext_count, inner), BF16), rows_spec(ext_len, inner)),
            (shape((ext_count, bc_width), BF16), rows_spec(ext_len, bc_width)),
            (shape((token_count, LANES), F32), aux_spec),
            (shape((token_count, inner), BF16), inner_spec),
            (shape((token_count, inner), BF16), inner_spec),
            (shape((token_count, bc_width), BF16), bc_spec),
            (shape((token_count, bc_width), BF16), bc_spec),
            (shape((token_count, 2 * LANES), F32), steps_spec),
            (shape((blocks, NS, inner), F32), state_spec),
            (shape((blocks, 8, inner), F32), batch_spec(8, inner)),
            (shape((8, width), F32), whole_spec(8, width)),
            (shape((width, pre_width), BF16), once_spec(width, pre_width)),
        ],
        [SMEM]
        + [ANY] * (2 * part_count)
        + [
            rows_spec(GHOST, width),
            rows_spec(length, width),
            aux_spec,
            whole_spec(8, inner),
            whole_spec(8, bc_width),
            params_spec,
        ],
        (
            places,
            *x_parts,
            *b_parts,
            tail,
            tokens.reshape(token_count, width),
            aux,
            conv_x_rows,
            conv_bc_rows,
            params,
        ),
        grid,
        scratch=[
            pltpu.VMEM((ext_len, inner), F32),
            pltpu.VMEM((ext_len, bc_width), F32),
            pltpu.VMEM((length, inner), BF16),
            pltpu.SemaphoreType.DMA,
        ],
        flops=2 * ext_count * width * (inner + rest_width),
        vmem=22,
    )
    (y_intra,) = kernel_call(
        intra_kernel,
        [(shape((token_count, inner), BF16), inner_spec)],
        [inner_spec, bc_spec, steps_spec, aux_spec, batch_spec(8, length), params_spec],
        (x_act, bc_act, steps, aux, seg_row, params),
        grid,
        flops=16 * token_count * length * inner,
    )
    z_parts, _ = gather_chunks(z_shard, z_came, b_far, late=chain)
    chunk_count = places.shape[0]
    each = chunk_count // part_count
    w_z, w_o = pl.pallas_call(
        functools.partial(order_kernel, part_count),
        grid_spec=pltpu.PrefetchScalarGridSpec(
            num_scalar_prefetch=1,
            grid=(chunk_count,),
            in_specs=[
                pl.BlockSpec(
                    (1, shard_rows, 2 * inner),
                    functools.partial(
                        lambda k, i, at: (jnp.clip(i - k * each, 0, each - 1), 0, 0), k
                    ),
                )
                for k in range(part_count)
            ],
            out_specs=[pl.BlockSpec((shard_rows, inner), lambda i, at: (at[i], 0))] * 2,
        ),
        out_shape=[shape((width, inner), BF16)] * 2,
        compiler_params=pltpu.CompilerParams(vmem_limit_bytes=8 * 2**20),
    )(places, *z_parts)
    gate_z = dot_nn(unit, w_z).astype(BF16)
    d_gnorm = dot_nn(flat_cot, w_o).astype(BF16)
    chain_row = chain[:, :1]
    state_in, state_out = state_scan(chain_row, local, False, ((), (y_intra, gate_z), (d_gnorm,)))
    ssd_out, scaled, own_sums = kernel_call(
        gated_kernel,
        [
            (shape((token_count, inner), F32), inner_spec),
            (shape((token_count, inner), BF16), inner_spec),
            (shape((blocks, 8, length), F32), batch_spec(8, length)),
        ],
        [
            inner_spec,
            bc_spec,
            state_spec,
            steps_spec,
            aux_spec,
            rows_spec(ext_len, inner),
            inner_spec,
            whole_spec(8, inner),
        ],
        (y_intra, bc_act, state_in, steps, aux, gate_z, d_gnorm, gains),
        grid,
        scratch=[pltpu.VMEM((length, inner), F32)],
        flops=2 * token_count * NS * inner,
    )
    (branch_part,) = kernel_call(
        branch_kernel,
        [
            (shape((token_count, width), BF16), pl.BlockSpec((token_count, tile), lambda i: (0, i)))
        ],
        [once_spec(token_count, inner), rows_spec(tile, inner)],
        (scaled, w_o),
        (tiles,),
        flops=2 * token_count * width * inner,
    )

    branch = lax.psum(branch_part, "tensor")
    own_sums = after(own_sums, branch_part)

    def backward():
        came_sums = fetch_tensor(own_sums)
        def half_call(body, start, filled, outs, shared, ins, args, scratch, flops, vmem=14):
            operands, specs, aliases = list(args), [spec(start) for spec in ins], {}
            if filled:
                aliases = {len(operands) + k: k for k in range(len(outs))}
                operands += filled
                specs += [ANY] * len(outs)
            made = kernel_call(
                body,
                [(o, spec(start)) for o, spec in outs] + list(shared),
                specs,
                operands,
                (halved,),
                scratch=scratch,
                aliases=aliases,
                flops=flops // 2,
                vmem=vmem,
            )
            return list(made[: len(outs)]), made[len(outs) :]

        def rows_from(rows, cols):
            return lambda start: rows_spec(rows, cols, start)

        def batch_from(rows, cols):
            return lambda start: batch_spec(rows, cols, start)

        def fixed(*dims):
            return lambda start: whole_spec(*dims)

        inner_from = rows_from(length, inner)
        bc_from = rows_from(length, bc_width)
        steps_from = rows_from(length, 2 * LANES)
        aux_from = rows_from(length, LANES)

        def intra_back(start, filled, token, d_ssd):
            return half_call(
                intra_back_kernel,
                start,
                filled,
                [
                    (shape((token_count, inner), BF16), inner_from),
                    (shape((token_count, bc_width), F32), bc_from),
                ],
                [],
                [inner_from, inner_from, bc_from, steps_from, aux_from, batch_from(8, length)],
                (d_ssd, x_act, bc_act, steps, aux, after(seg_row, *token)),
                [],
                32 * token_count * length * inner,
            )[0]

        def last(start, filled, token):
            return half_call(
                last_kernel,
                start,
                filled,
                [(shape((ext_count, pre_width), BF16), rows_from(ext_len, pre_width))],
                [
                    (shape((8, inner), F32), whole_spec(8, inner)),
                    (shape((8, bc_width), F32), whole_spec(8, bc_width)),
                    (shape((8, LANES), F32), params_spec),
                ],
                [
                    batch_from(NS, inner),
                    batch_from(NS, inner),
                    batch_from(NS, inner),
                    inner_from,
                    inner_from,
                    inner_from,
                    bc_from,
                    steps_from,
                    aux_from,
                    aux_from,
                    inner_from,
                    bc_from,
                    rows_from(ext_len, inner),
                    rows_from(ext_len, bc_width),
                    inner_from,
                    bc_from,
                    fixed(8, inner),
                    fixed(8, bc_width),
                    fixed(8, LANES),
                ],
                (
                    state_back,
                    state_in,
                    state_out,
                    d_ssd,
                    x_act,
                    ssd_out,
                    bc_act,
                    steps,
                    dt_raw,
                    aux,
                    d_x_dt,
                    d_bc,
                    x_ext,
                    bc_ext,
                    x_slope,
                    bc_slope,
                    conv_x_rows,
                    conv_bc_rows,
                    after(params, *token),
                ),
                [
                    pltpu.VMEM((ext_len, inner), F32),
                    pltpu.VMEM((ext_len, bc_width), F32),
                    pltpu.VMEM((ext_len, LANES), F32),
                    pltpu.VMEM((length, inner), F32),
                ]
                + [pltpu.VMEM((length, inner), BF16)] * 6,
                8 * token_count * NS * inner,
                22,
            )

        d_ssd, d_gate, g_norm, state_grad, scales, grad_out_gain = kernel_call(
            functools.partial(back_kernel, tensor_count),
            [
                (shape((token_count, inner), BF16), inner_spec),
                (shape((ext_count, inner), BF16), rows_spec(ext_len, inner)),
                (shape((token_count, inner), BF16), inner_spec),
                (shape((blocks, NS, inner), F32), state_spec),
                (shape((token_count, LANES), F32), aux_spec),
                (shape((8, inner), F32), whole_spec(8, inner)),
            ],
            [SMEM]
            + [batch_spec(8, length)] * tensor_count
            + [
                inner_spec,
                rows_spec(ext_len, inner),
                inner_spec,
                steps_spec,
                aux_spec,
                bc_spec,
                whole_spec(8, inner),
            ],
            (me, own_sums, *came_sums, ssd_out, gate_z, d_gnorm, steps, aux, bc_act, gains),
            grid,
            scratch=[pltpu.VMEM((length, inner), BF16)],
            flops=2 * token_count * NS * inner,
        )

        first = intra_back(0, None, (), d_ssd)
        d_x_dt, d_bc = intra_back(halved, first, (), d_ssd)
        state_back, _ = state_scan(chain_row, state_grad, True, ((first[1],), (d_bc,)))
        first_pre, first_grads = last(0, None, ())
        (d_pre,), last_grads = last(halved, first_pre, ())
        d_unit = (dot_nt(d_gate, w_z) + dot_nt(d_pre, w_pre)).astype(BF16)
        ghost = d_unit.reshape(blocks, ext_len, width)[:, :GHOST].reshape(blocks * GHOST, width)
        from_next = lax.ppermute(ghost, "seq", [(i + 1, i) for i in range(seq_count - 1)])
        d_parts = kernel_call(
            mains_kernel,
            [(shape((length, width), BF16), pl.BlockSpec((length, tile), lambda i: (0, i)))]
            * blocks,
            [
                pl.BlockSpec((ext_count, tile), lambda i: (0, i)),
                pl.BlockSpec((blocks * GHOST, tile), lambda i: (0, i)),
            ],
            (d_unit, from_next),
            (tiles,),
        )
        return d_gate, d_pre, g_norm, scales, d_parts, grad_out_gain, first_grads, last_grads

    d_gate, d_pre, g_norm, scales, d_parts, grad_out_gain, first_grads, last_grads = in_turn(
        me, (branch_part,), backward
    )

    def weight_grad(*pairs):
        found = [
            lax.dot_general(
                left, right, (((0,), (0,)), ((), ())), preferred_element_type=F32
            ).astype(BF16)
            for left, right in pairs
        ]
        columns = sum(f.shape[1] for f in found)

        def chunks(low, high):
            return pl.pallas_call(
                copy_kernel,
                grid_spec=pltpu.PrefetchScalarGridSpec(
                    num_scalar_prefetch=1,
                    grid=(high - low,),
                    in_specs=[
                        pl.BlockSpec((shard_rows, f.shape[1]), lambda i, at: (at[i], 0))
                        for f in found
                    ],
                    out_specs=pl.BlockSpec((1, shard_rows, columns), lambda i, at: (i, 0, 0)),
                ),
                out_shape=shape((high - low, shard_rows, columns), BF16),
                compiler_params=pltpu.CompilerParams(vmem_limit_bytes=8 * 2**20),
            )(places[low:high], *found)

        if not is_grid():
            return (chunks(0, chunk_count),) * 2
        return chunks(4, 8), chunks(0, 4)

    small = jnp.concatenate(
        [
            first_grads[0] + last_grads[0],
            grad_out_gain,
            first_grads[1] + last_grads[1],
            first_grads[2] + last_grads[2],
        ],
        axis=1,
    )

    def products():
        return sum_cores(*weight_grad((unit, d_gate), (unit, d_pre), (flat_cot, g_norm)))

    kept, away = in_turn(me, d_parts, products)
    branch = after(branch, away)

    line = tensor_count == 4
    step = length // 4
    flat_tokens = tokens.reshape(token_count, width)

    def start(hop, value):
        return hop(value) if line else value

    def arrived(kept, came, token):
        return low_sum(kept, after(came, token)) if line else kept

    def finish_grad(b, filled, token):
        placed = rows_spec(step, width, 4 * b)
        here = rows_spec(step, width)
        back = after(outs[b], token)
        operands = [at_edge, totals[b], back, flat_tokens, flat_cot, gain_row]
        ins = [SMEM, here, here, placed, placed, whole_spec(8, width)]
        aliases = {}
        if filled is not None:
            aliases = {len(operands): 0}
            operands.append(filled)
            ins.append(ANY)
        (found,) = kernel_call(
            token_grad_kernel,
            [(shape((token_count, width), F32), placed)],
            ins,
            operands,
            (4,),
            aliases=aliases,
        )
        return found

    parts = [after(part, branch) for part in d_parts]
    if not line:
        parts = [lax.psum(part, "tensor") for part in parts]
    inward = [start(hop_in, part) for part in parts[:2]]
    wide_spec = rows_spec(length // 2, width)
    (output,) = kernel_call(
        output_kernel,
        [(shape((token_count, width), BF16), wide_spec)],
        [wide_spec, wide_spec, rows_spec(length // 2, LANES)],
        (branch, flat_tokens, scales),
        (2 * blocks,),
    )
    halves = [arrived(parts[0], inward[0], output)]
    across = [start(hop_across, halves[0])]
    inward.append(start(hop_in, after(parts[2], halves[0])))
    small = small + after(swap(small, "seq", 1), halves[0])
    halves.append(arrived(parts[1], inward[1], halves[0]))
    across.append(start(hop_across, halves[1]))
    inward.append(start(hop_in, after(parts[3], halves[1])))
    totals = [arrived(halves[0], across[0], halves[1])]
    outs = [start(hop_out, totals[0])]
    kept, away = sum_second(kept, away, totals[0])
    small = small + after(swap(small, "seq", 2), totals[0])
    halves.append(arrived(parts[2], inward[2], away))
    across.append(start(hop_across, halves[2]))
    totals.append(arrived(halves[1], across[1], halves[2]))
    outs.append(start(hop_out, totals[1]))
    small = small_sum(small, ("dp",))
    token_grad = finish_grad(0, None, after(small, totals[1]))
    halves.append(arrived(parts[3], inward[3], token_grad))
    across.append(start(hop_across, halves[3]))
    totals.append(arrived(halves[2], across[2], halves[3]))
    outs.append(start(hop_out, totals[2]))
    token_grad = finish_grad(1, token_grad, totals[2])
    grads = sum_first(kept, away, token_grad)
    bc_part = grads[:, 2 * inner : 2 * inner + bc_width]
    bc_part = jnp.swapaxes(bc_part.reshape(shard_rows, tensor_count, bc_own), 0, 1)
    gain_part = (
        jnp.sum(grads[:, :inner] * z_proj.astype(F32), axis=1)
        + jnp.sum(grads[:, inner : 2 * inner] * x_proj.astype(F32), axis=1)
        + jnp.sum(grads[:, 2 * inner : inner + pre_width] * rest_shard.astype(F32), axis=1)
    )
    gain_part = jnp.pad(gain_part, (0, bc_width - shard_rows))[None]
    bc_sums = small[: KW + 1, 2 * inner : 2 * inner + bc_width]
    bc_sums = jnp.concatenate([bc_sums, gain_part, jnp.zeros((2, bc_width), F32)])
    totals.append(arrived(halves[3], across[3], bc_sums))
    outs.append(start(hop_out, totals[3]))
    token_grad = finish_grad(2, token_grad, totals[3])
    grad_bc, shared = sum_tensor(bc_part, bc_sums, token_grad)
    token_grad = finish_grad(3, token_grad, shared)
    grad_z, grad_x = grads[:, :inner], grads[:, inner : 2 * inner]
    grad_dt = grads[:, 2 * inner + bc_width : 2 * inner + bc_width + heads]
    grad_out = grads[:, inner + pre_width :].T
    x_sums = small[:, :inner]
    head_sums = small[:, 2 * inner + bc_width :]
    bc_mine = lax.dynamic_slice_in_dim(shared[: KW + 1], tensor_pos * bc_own, bc_own, 1)
    return (
        output.reshape(tokens.shape),
        token_grad.reshape(tokens.shape),
        shared[KW + 1, :shard_rows] / in_gain.astype(F32),
        grad_z,
        grad_x,
        grad_bc,
        grad_dt,
        grad_out,
        x_sums[:KW],
        x_sums[KW],
        bc_mine[:KW],
        bc_mine[KW],
        head_sums[0, :heads],
        head_sums[1, :heads],
        jnp.sum(x_sums[KW + 1].reshape(heads, HD), axis=1),
        small[0, inner : 2 * inner],
    )


def solution(mesh):
    in_specs = (
        P(None, "dp", "seq", None),
        P(None, "dp", None),
        P(None, "dp", "seq", None),
        P(("dp", "seq")),
        P(("dp", "seq"), "tensor"),
        P(("dp", "seq"), "tensor"),
        P(("dp", "seq"), "tensor"),
        P(("dp", "seq"), "tensor"),
        P("tensor", ("dp", "seq")),
        P(None, "tensor"),
        P("tensor"),
        P(None, "tensor"),
        P("tensor"),
        P("tensor"),
        P("tensor"),
        P("tensor"),
        P("tensor"),
    )
    out_specs = (
        P(None, "dp", "seq", None),
        P(None, "dp", "seq", None),
        P(("dp", "seq")),
        P(("dp", "seq"), "tensor"),
        P(("dp", "seq"), "tensor"),
        P(("dp", "seq"), "tensor"),
        P(("dp", "seq"), "tensor"),
        P("tensor", ("dp", "seq")),
        P(None, "tensor"),
        P("tensor"),
        P(None, "tensor"),
        P("tensor"),
        P("tensor"),
        P("tensor"),
        P("tensor"),
        P("tensor"),
    )
    return jax.shard_map(
        per_device, mesh=mesh, in_specs=in_specs, out_specs=out_specs, check_vma=False
    )
```
